32 devices in a mesh: req: 4 (over z), blk: 8 (over y, x, core).
Axes of the slice: x: 2, y: 2, z: 4, core: 2. Of those that a mesh axis runs over, the one named last changes fastest.
Arguments:
- tree_input: bfloat16 [1536, 1280], P(('req', 'blk')), may hold values from -6 to 6
- cache: bfloat16 [4, 2, 16384, 1280], P('req', None, 'blk'), may hold values from -1200 to 1200, as said below
- page_table: int32 [4, 128], P('req'), may hold values from 0 to 127, each once within a row
- lengths: int32 [4, 8], P('req'), may hold values from 1 to 13440, 14336 in all within a row
- parents: int32 [32, 48], P(('req', 'blk')), may hold values from 0 to 29, as said below
- accept_leaf: int32 [4, 8], P('req'), may hold values from 0 to 47
- w_qkv: bfloat16 [1280, 3840], P(None, 'blk'), may hold values from -0.15625 to 0.15625
- w_out: bfloat16 [1280, 1280], P(None, 'blk'), may hold values from -0.15625 to 0.15625
- w_up: bfloat16 [1280, 1280], P(None, 'blk'), may hold values from -0.15625 to 0.15625
- w_down: bfloat16 [1280, 1280], P('blk'), may hold values from -0.15625 to 0.15625
- w_draft: bfloat16 [4, 1280, 1280], P(None, None, 'blk'), may hold values from -0.15625 to 0.15625
- w_patch: bfloat16 [1280, 1280], P(None, 'req'), may hold values from -0.15625 to 0.15625
Outputs:
- layer_out: bfloat16 [1536, 1280], P(('req', 'blk'))
- drafts: bfloat16 [4, 1536, 1280], P(None, ('req', 'blk'))
- cache_new: bfloat16 [4, 2, 16384, 1280], P('req', None, 'blk')
The draws below stay inside these ranges and needn't reach their ends.
Inputs may be any that keep to these rules, and one draw needn't show every extreme that they name: `cache`: keys of the pool may hold a few rows of far larger size. `parents`: node 0 is its own parent. The nodes form 5 levels of sizes 1, 4, 10, 15, 18 in index order, and every other node's parent lies in the level before its own. `page_table`: row g holds the pool pages of group g; request r's pages are the npages_r entries after those of requests before it (see the steps), and page p is held by index p // 16 of blk.
All inputs are finite; a program needn't handle non-finite values.
Results may differ from the reference program's by a relative error of at most 0.018.
The reference program's roundings to bfloat16 on the way count: a program that leaves them out, or rounds other values in their place, can miss the bound.
Values may be sent and summed in bfloat16 or wider, within the bound.
No kernel may reach another device: no remote copies, remote signals or barrier semaphores. Data moves between devices by JAX's collectives and lax.ppermute only.
A program may use at most 192 MiB of HBM per device.

```python
import math
import jax
import jax.numpy as jnp
import numpy as np
from jax import lax

D = 1280
H = 16
HD = 80
FF = 1280
OUTW = 1280
KHEADS = 4
TREE = 48
DEPTH = 5
PAGE = 128
GROUP_REQS = 8
REQS = 32
ROWS = 1536
POOL_PAGES = 128
SLOTS = 16384
LEN_TOTAL = 14336
MAXLEN = 13440
N_REQ = 4


def draw_cache(key, part):
    shape = (N_REQ, 2, SLOTS, D)
    base = jnp.clip(jax.random.normal(jax.random.fold_in(key, 11), shape, jnp.float32), -6.0, 6.0)
    key_side = (jnp.arange(2) == 0).reshape(1, 2, 1, 1)
    base = base * jnp.where(key_side, 2.5, 1.0)
    return base.astype(jnp.bfloat16)


def draw_parents(key, part):
    starts = np.array([0, 1, 5, 15, 30, 48])
    level = np.searchsorted(starts, np.arange(48), side='right') - 1
    lowest = np.where(level > 0, starts[np.maximum(level - 1, 0)], 0)
    spread = np.where(level > 0, starts[level] - lowest, 1)
    offset = jax.random.randint(jax.random.fold_in(key, 17), (REQS, TREE), 0, 1 << 20)
    return (jnp.asarray(lowest, jnp.int32)[None, :] + offset % jnp.asarray(spread, jnp.int32)[None, :]).astype(jnp.int32)


def plant(entries, rng, low, largest):
    spot = [jax.random.randint(jax.random.fold_in(rng, axis), (), 0, length) for axis, length in enumerate(entries.shape)]
    widest = entries.shape.index(max(entries.shape))
    beside = spot[:widest] + [(spot[widest] + 1) % entries.shape[widest]] + spot[widest + 1:]
    return entries.at[tuple(spot)].set(low).at[tuple(beside)].set(largest)


def levels(rng, extent, shards, least, largest):
    def one(axis_at, parts):
        steps = jax.random.uniform(jax.random.fold_in(jax.random.fold_in(rng, 6), axis_at), (parts,), jnp.float32, least / len(shards), largest / len(shards))
        return jnp.repeat(jnp.exp(steps), extent[axis_at] // parts).reshape((-1,) + (1,) * (len(extent) - axis_at - 1))

    gain = one(*shards[0])
    for cut in shards[1:]:
        gain = gain * one(*cut)
    return gain


def profile(number_of, total, most, lean):
    portions = [(1 << 20) // math.isqrt(grade ** lean) + 1 for grade in range(2, number_of + 1)]
    surplus, counts = total - most - (number_of - 1), [1] * (number_of - 1)
    while surplus > 0:
        movable = [i for i in range(number_of - 1) if counts[i] < most]
        whole, left = sum([portions[i] for i in movable]), surplus
        for i in movable:
            extra = min(most - counts[i], max(1, left * portions[i] // whole), surplus)
            counts[i] = counts[i] + extra
            surplus = surplus - extra
    return np.array([most] + counts)


def ragged(stream_key, count, total, reach, slope):
    if count == 2:
        one = jax.random.randint(stream_key, (), max(1, total - reach), min(reach, total - 1) + 1)
        return jnp.stack([one, total - one])
    sizes = jnp.asarray(profile(count, total, reach, slope), jnp.int32)
    twos = (count - 1) // 2
    source_of, sink = sizes[1:1 + 2 * twos:2], sizes[2:2 + 2 * twos:2]
    margin = jnp.minimum(source_of - 1, reach - sink)
    shifted = jax.random.randint(jax.random.fold_in(stream_key, 1), (twos,), 0, 1 << 20) % (margin + 1)
    sizes = sizes.at[1:1 + 2 * twos:2].set(source_of - shifted).at[2:2 + 2 * twos:2].set(sink + shifted)
    return sizes[jax.random.permutation(jax.random.fold_in(stream_key, 2), count)]


def noise(key, dims, scale, most, cuts=(), kind=jnp.bfloat16):
    gain = levels(key, dims, cuts, -0.22, 0.18) if cuts else 1.0
    values = jax.random.normal(key, dims, jnp.float32) * scale * gain
    return jnp.minimum(jnp.maximum(values, -most), most).astype(kind)


def setup_inputs(seed: int = 0) -> dict:
    splits = jax.random.split(jax.random.key(seed), 13)
    tree_input = noise(splits[0], (ROWS, D), 1.0, 6.0, ((0, 32),))
    cache = draw_cache(jax.random.fold_in(splits[12], 71), 0)
    page_table = jax.vmap(lambda own: jax.random.permutation(own, POOL_PAGES))(jax.random.split(splits[2], N_REQ)).reshape((N_REQ, POOL_PAGES)).astype(jnp.int32)
    lengths = jax.vmap(lambda own: ragged(own, GROUP_REQS, LEN_TOTAL, MAXLEN, 2))(jax.random.split(splits[3], N_REQ)).reshape((N_REQ, GROUP_REQS)).astype(jnp.int32)
    parents = draw_parents(jax.random.fold_in(splits[12], 71), 0)
    accept_leaf = plant(jax.random.randint(splits[5], (N_REQ, GROUP_REQS), 0, TREE), jax.random.fold_in(splits[5], 1), 0, TREE - 1).astype(jnp.int32)
    w_qkv = noise(splits[6], (D, 3 * D), D ** -0.5, 0.15625, ((1, 8),))
    w_out = noise(splits[7], (D, D), D ** -0.5, 0.15625, ((1, 8),))
    w_up = noise(splits[8], (D, FF), D ** -0.5, 0.15625, ((1, 8),))
    w_down = noise(splits[9], (FF, D), FF ** -0.5, 0.15625, ((0, 8),))
    w_draft = noise(splits[10], (KHEADS, D, D), D ** -0.5, 0.15625, ((2, 8),))
    w_patch = noise(splits[11], (D, OUTW), D ** -0.5, 0.15625, ((1, 4),))
    return {"tree_input": tree_input, "cache": cache, "page_table": page_table, "lengths": lengths, "parents": parents, "accept_leaf": accept_leaf, "w_qkv": w_qkv, "w_out": w_out, "w_up": w_up, "w_down": w_down, "w_draft": w_draft, "w_patch": w_patch}


EPS = 1e-06
NEG = -1e+30

def rms_rows(values):
    wide = values.astype(jnp.float32)
    return (wide * lax.rsqrt(lax.optimization_barrier(jnp.mean(wide * wide, axis=-1, keepdims=True)) + EPS)).astype(jnp.bfloat16)

def ancestors(parent_rows):
    nodes = jnp.arange(TREE, dtype=jnp.int32)
    current = jnp.broadcast_to(nodes, parent_rows.shape).astype(jnp.int32)
    marks = current[:, :, None] == nodes[None, None, :]
    for level in range(DEPTH - 1):
        current = jnp.take_along_axis(parent_rows, current, axis=1)
        marks = marks | (current[:, :, None] == nodes[None, None, :])
    return marks

def group_step(inputs):
    query, key_new, value_new, pool, page_row, length_row, parent_rows, leaf_row = inputs
    requests = length_row.shape[0]
    pool_count = page_row.shape[0]
    scale = 1.0 / math.sqrt(HD)
    npages = (length_row + DEPTH + PAGE - 1) // PAGE
    page_ends = jnp.cumsum(npages).astype(jnp.int32)
    offsets = (page_ends - npages).astype(jnp.int32)
    inverse = jnp.zeros((pool_count,), jnp.int32).at[page_row].set(jnp.arange(pool_count, dtype=jnp.int32))
    owner = lax.optimization_barrier(jnp.sum((page_ends[None, :] <= inverse[:, None]).astype(jnp.int32), axis=1))
    owner_hot = owner[:, None] == jnp.arange(requests, dtype=jnp.int32)[None, :]
    safe_owner = jnp.minimum(owner, requests - 1)
    page_len = jnp.where(owner < requests, length_row[safe_owner], 0)
    page_slot = inverse - offsets[safe_owner]
    positions = page_slot[:, None] * PAGE + jnp.arange(PAGE, dtype=jnp.int32)[None, :]
    valid = positions < page_len[:, None]
    query4 = query.reshape(requests, TREE, H, HD).astype(jnp.float32)
    keys = pool[0].reshape(pool_count, PAGE, H, HD).astype(jnp.float32)
    values = pool[1].reshape(pool_count, PAGE, H, HD).astype(jnp.float32)
    query_page = query4[safe_owner]
    scores = jnp.einsum('pqhd,pthd->pqht', query_page, keys, precision=lax.Precision.HIGHEST) * scale
    masked = jnp.where(valid[:, None, None, :], scores, NEG)
    page_max = lax.optimization_barrier(jnp.max(masked, axis=-1))
    cache_max = lax.optimization_barrier(jnp.max(jnp.where(owner_hot[:, :, None, None], page_max[:, None], NEG), axis=0))
    key4 = key_new.reshape(requests, TREE, H, HD).astype(jnp.float32)
    value4 = value_new.reshape(requests, TREE, H, HD).astype(jnp.float32)
    marks = ancestors(parent_rows)
    tree_scores = jnp.einsum('rqhd,rkhd->rqhk', query4, key4, precision=lax.Precision.HIGHEST) * scale
    tree_masked = jnp.where(marks[:, :, None, :], tree_scores, NEG)
    row_top = jnp.maximum(cache_max, lax.optimization_barrier(jnp.max(tree_masked, axis=-1)))
    page_top = row_top[safe_owner]
    weights = jnp.where(valid[:, None, None, :], jnp.exp(masked - page_top[..., None]), 0.0)
    weights_low = lax.optimization_barrier(weights.astype(jnp.bfloat16)).astype(jnp.float32)
    hot = owner_hot.astype(jnp.float32)
    cache_den = jnp.einsum('pr,pqh->rqh', hot, lax.optimization_barrier(jnp.sum(weights, axis=-1)), precision=lax.Precision.HIGHEST)
    page_num = jnp.einsum('pqht,pthd->pqhd', weights_low, values, precision=lax.Precision.HIGHEST)
    cache_num = jnp.einsum('pr,pqhd->rqhd', hot, page_num, precision=lax.Precision.HIGHEST)
    tree_weights = jnp.where(marks[:, :, None, :], jnp.exp(tree_masked - row_top[..., None]), 0.0)
    tree_low = lax.optimization_barrier(tree_weights.astype(jnp.bfloat16)).astype(jnp.float32)
    denom = cache_den + lax.optimization_barrier(jnp.sum(tree_weights, axis=-1))
    numer = cache_num + jnp.einsum('rqhk,rkhd->rqhd', tree_low, value4, precision=lax.Precision.HIGHEST)
    attended = (numer / denom[..., None]).reshape(requests * TREE, H * HD).astype(jnp.bfloat16)
    chosen = marks[jnp.arange(requests), leaf_row]
    ranks = jnp.cumsum(chosen.astype(jnp.int32), axis=1) - 1
    written = length_row[:, None] + ranks
    page_index = page_row[jnp.clip(offsets[:, None] + written // PAGE, 0, pool_count - 1)]
    target = jnp.where(chosen, page_index * PAGE + written % PAGE, pool_count * PAGE).reshape(-1)
    new_keys = pool[0].at[target].set(key_new, mode='drop')
    new_values = pool[1].at[target].set(value_new, mode='drop')
    return (attended, jnp.stack([new_keys, new_values]))

def reference(tree_input, cache, page_table, lengths, parents, accept_leaf, w_qkv, w_out, w_up, w_down, w_draft, w_patch):
    width = tree_input.shape[1]
    groups = lengths.shape[0]
    normed = rms_rows(tree_input)
    projected = jnp.dot(normed, w_qkv, preferred_element_type=jnp.float32).astype(jnp.bfloat16)

    def by_group(block):
        return block.reshape(groups, -1, block.shape[-1])
    attended, cache_new = lax.map(group_step, (by_group(projected[:, :width]), by_group(projected[:, width:2 * width]), by_group(projected[:, 2 * width:]), cache, page_table, lengths, parents.reshape(groups, -1, TREE), accept_leaf))
    attended = attended.reshape(-1, width)
    proj = jnp.dot(attended, w_out, preferred_element_type=jnp.float32).astype(jnp.bfloat16)
    mid = (tree_input.astype(jnp.float32) + proj.astype(jnp.float32)).astype(jnp.bfloat16)
    hidden = jax.nn.gelu(jnp.dot(rms_rows(mid), w_up, preferred_element_type=jnp.float32)).astype(jnp.bfloat16)
    layer_out = (mid.astype(jnp.float32) + jnp.dot(hidden, w_down, preferred_element_type=jnp.float32)).astype(jnp.bfloat16)
    draft_normed = rms_rows(layer_out)
    branch = jax.nn.silu(jnp.einsum('nd,kdc->knc', draft_normed.astype(jnp.float32), w_draft.astype(jnp.float32))).astype(jnp.bfloat16)
    drafted = (layer_out.astype(jnp.float32)[None] + branch.astype(jnp.float32)).astype(jnp.bfloat16)
    drafts = jnp.einsum('knd,do->kno', drafted.astype(jnp.float32), w_patch.astype(jnp.float32)).astype(jnp.bfloat16)
    return (layer_out, drafts, cache_new)
```

```python
import functools
import math

import jax
import jax.numpy as jnp
from jax import lax
from jax.experimental import pallas as pl
from jax.experimental.pallas import tpu as pltpu
from jax.sharding import PartitionSpec as P

H = 16
HD = 80
TREE = 48
DEPTH = 5
PAGE = 128
EPS = 1e-06
NEG = -1e30
LEVEL_START = (0, 1, 5, 15, 30, 48)
SCALE = 1.0 / math.sqrt(HD)

WIN = 256
WINDOWS = H * HD // WIN
SLOTS = 4
LOW = 16
SIDE = 128
SHARDS_AT = (0, 2, 4, 6, 1, 3, 5, 7)
LIGHT = pl.CostEstimate(flops=0, bytes_accessed=0, transcendentals=0)
HBM = pl.BlockSpec(memory_space=pltpu.HBM)


def rms_rows(values):
    wide = values.astype(jnp.float32)
    return (wide * lax.rsqrt(jnp.mean(wide * wide, axis=-1, keepdims=True) + EPS)).astype(
        jnp.bfloat16
    )


def dot_t(left, right):
    return lax.dot_general(
        left, right, (((1,), (1,)), ((), ())), preferred_element_type=jnp.float32
    )


def dot_n(left, right):
    return lax.dot_general(
        left, right, (((1,), (0,)), ((), ())), preferred_element_type=jnp.float32
    )


def in_head(window, slot, rows):
    lane = lax.broadcasted_iota(jnp.int32, (rows, WIN), 1)
    first = (3 * window + slot) * HD - window * WIN
    return (lane >= first) & (lane < first + HD)


def masked_queries(rows, window):
    part = rows[:, window * WIN : (window + 1) * WIN].astype(jnp.float32)
    slots = [
        jnp.where(in_head(window, slot, TREE), part, 0.0).astype(jnp.bfloat16)
        for slot in range(SLOTS)
    ]
    return jnp.concatenate(slots, axis=0)


def by_head(products):
    pieces = [None] * H
    for window, product in enumerate(products):
        for slot in range(SLOTS):
            piece = product[slot * TREE : (slot + 1) * TREE]
            head = 3 * window + slot
            pieces[head] = piece if pieces[head] is None else pieces[head] + piece
    return pieces


def own_lanes(product, window):
    total = None
    for slot in range(SLOTS):
        piece = jnp.where(
            in_head(window, slot, TREE), product[slot * TREE : (slot + 1) * TREE], 0.0
        )
        total = piece if total is None else total + piece
    return total


def heads_to_lanes(column):
    lane = lax.broadcasted_iota(jnp.int32, (TREE, SIDE), 1) & (H - 1)
    total = jnp.zeros((TREE, SIDE), jnp.float32)
    for head in range(H):
        total = jnp.where(lane == head, column[head * TREE : (head + 1) * TREE], total)
    return total


def three_parts(wide):
    lane = lax.broadcasted_iota(jnp.int32, wide.shape, 1)
    high = wide.astype(jnp.bfloat16).astype(jnp.float32)
    rest = wide - high
    middle = rest.astype(jnp.bfloat16).astype(jnp.float32)
    low = rest - middle
    return jnp.where(
        lane < 32, high, jnp.where(lane < 64, middle, jnp.where(lane < 96, low, 0.0))
    ).astype(jnp.bfloat16)


def attend_body(
    pages,
    requests,
    info,
    q_ref,
    cache_ref,
    part_ref,
    copy_ref,
    held,
    scores,
    queries,
    top,
    total,
    numer,
    load_sem,
    save_sem,
):
    width = q_ref.shape[1]

    def place(page):
        return pl.ds(pl.multiple_of(info[page] * PAGE, PAGE), PAGE)

    def load(side, page):
        return pltpu.make_async_copy(
            cache_ref.at[side, place(page)], held.at[side, page], load_sem.at[side, page]
        )

    def save(side, page):
        return pltpu.make_async_copy(
            held.at[side, page], copy_ref.at[side, place(page)], save_sem.at[side, page]
        )

    for side in range(2):
        for page in range(pages):
            load(side, page).start()

    def request(r, carry):
        begin = info[2 * pages + r]
        count = info[2 * pages + requests + r]

        @pl.when(count == 0)
        def _():
            part_ref[r, :, :width] = jnp.zeros((TREE, width), jnp.bfloat16)
            part_ref[r, :, width:] = three_parts(jnp.full((TREE, SIDE), NEG, jnp.float32))

        @pl.when(count > 0)
        def _():
            rows = q_ref[pl.ds(pl.multiple_of(r * TREE, 16), TREE), :]
            for window in range(WINDOWS):
                queries[window] = masked_queries(rows, window)
            top[...] = jnp.full(top.shape, NEG, jnp.float32)

            def score(i, carry):
                page = begin + i
                load(0, page).wait()
                save(0, page).start()
                keep = lax.broadcasted_iota(jnp.int32, (TREE, PAGE), 1) < info[pages + page]
                products = [
                    dot_t(
                        queries[window], held[0, page, :, window * WIN : (window + 1) * WIN]
                    )
                    for window in range(WINDOWS)
                ]
                for head, piece in enumerate(by_head(products)):
                    span = pl.ds(head * TREE, TREE)
                    masked = jnp.where(keep, piece * SCALE, NEG)
                    scores[page, span] = masked
                    top[span] = jnp.maximum(top[span], masked)
                return carry

            lax.fori_loop(0, count, score, 0)
            largest = jnp.max(top[...], axis=1, keepdims=True)
            top[...] = jnp.broadcast_to(largest, top.shape)
            total[...] = jnp.zeros(total.shape, jnp.float32)
            numer[...] = jnp.zeros(numer.shape, jnp.float32)

            def weigh(i, carry):
                page = begin + i
                load(1, page).wait()
                save(1, page).start()
                weights = jnp.exp(scores[page] - top[...])
                total[...] += weights
                low = weights.astype(jnp.bfloat16)
                for window in range(WINDOWS):
                    first = 3 * window * TREE
                    numer[window] += dot_n(
                        low[first : first + SLOTS * TREE],
                        held[1, page, :, window * WIN : (window + 1) * WIN],
                    )
                return carry

            lax.fori_loop(0, count, weigh, 0)
            denom = jnp.sum(total[...], axis=1, keepdims=True)
            inverse = 1.0 / denom
            for window in range(WINDOWS):
                first = 3 * window * TREE
                scaled = numer[window] * inverse[first : first + SLOTS * TREE]
                part_ref[r, :, window * WIN : (window + 1) * WIN] = own_lanes(
                    scaled, window
                ).astype(jnp.bfloat16)
            part_ref[r, :, width:] = three_parts(
                heads_to_lanes(top[:, :1] + jnp.log(denom))
            )

        return carry

    lax.fori_loop(0, requests, request, 0)
    used = info[2 * pages + requests - 1] + info[2 * pages + 2 * requests - 1]

    def untouched(page, carry):
        for side in range(2):
            load(side, page).wait()
            save(side, page).start()
        return carry

    lax.fori_loop(used, pages, untouched, 0)

    def settle(page, carry):
        for side in range(2):
            save(side, page).wait()
        return carry

    lax.fori_loop(0, pages, settle, 0)


def attend(info, query_all, cache, requests):
    pages = cache.shape[1] // PAGE
    width = query_all.shape[1]
    return pl.pallas_call(
        functools.partial(attend_body, pages, requests),
        out_shape=(
            jax.ShapeDtypeStruct((requests, TREE, width + SIDE), jnp.bfloat16),
            jax.ShapeDtypeStruct(cache.shape, cache.dtype),
        ),
        in_specs=[
            pl.BlockSpec(memory_space=pltpu.SMEM),
            pl.BlockSpec(memory_space=pltpu.VMEM),
            HBM,
        ],
        out_specs=(
            pl.BlockSpec(memory_space=pltpu.VMEM),
            HBM,
        ),
        scratch_shapes=[
            pltpu.VMEM((2, pages, PAGE, width), jnp.bfloat16),
            pltpu.VMEM((pages, H * TREE, PAGE), jnp.float32),
            pltpu.VMEM((WINDOWS, SLOTS * TREE, WIN), jnp.bfloat16),
            pltpu.VMEM((H * TREE, PAGE), jnp.float32),
            pltpu.VMEM((H * TREE, PAGE), jnp.float32),
            pltpu.VMEM((WINDOWS, SLOTS * TREE, WIN), jnp.float32),
            pltpu.SemaphoreType.DMA((2, pages)),
            pltpu.SemaphoreType.DMA((2, pages)),
        ],
        compiler_params=pltpu.CompilerParams(vmem_limit_bytes=60 * 1024 * 1024),
        cost_estimate=pl.CostEstimate(
            flops=4 * pages * PAGE * H * TREE * WIN,
            bytes_accessed=5 * cache.size,
            transcendentals=pages * PAGE * H * TREE,
        ),
        name="attend",
    )(info, query_all, cache)


def project_body(tree_ref, w_ref, out_ref):
    blocks = out_ref.shape[0]
    product = dot_t(rms_rows(tree_ref[...]), w_ref[...]).astype(jnp.bfloat16)
    for block in range(blocks):
        out_ref[block] = product[block * TREE : (block + 1) * TREE]


def project(tree_all, w_rows):
    rows, width = tree_all.shape
    columns = w_rows.shape[0]
    return pl.pallas_call(
        project_body,
        out_shape=jax.ShapeDtypeStruct((rows // TREE, TREE, columns), jnp.bfloat16),
        in_specs=[pl.BlockSpec(memory_space=pltpu.VMEM)] * 2,
        out_specs=pl.BlockSpec(memory_space=pltpu.VMEM),
        compiler_params=pltpu.CompilerParams(vmem_limit_bytes=24 * 1024 * 1024),
        cost_estimate=LIGHT,
        name="project",
    )(tree_all, w_rows)


def tree_body(info, qkv_ref, parent_ref, part_ref, send_ref):
    width = qkv_ref.shape[1] // 3
    node_row = lax.broadcasted_iota(jnp.int32, (TREE, TREE), 0)
    node_col = lax.broadcasted_iota(jnp.int32, (TREE, TREE), 1)
    steps = jnp.minimum(parent_ref[...] + jnp.where(node_row == node_col, 1.0, 0.0), 1.0)
    for _ in range(2):
        low = steps.astype(jnp.bfloat16)
        steps = jnp.minimum(dot_n(low, low), 1.0)
    marks = steps > 0.5

    query = qkv_ref[:, :width]
    key = qkv_ref[:, width : 2 * width]
    value = qkv_ref[:, 2 * width :]
    products = [
        dot_t(masked_queries(query, window), key[:, window * WIN : (window + 1) * WIN])
        for window in range(WINDOWS)
    ]
    scores = jnp.concatenate(
        [jnp.where(marks, piece * SCALE, NEG) for piece in by_head(products)], axis=0
    )
    top = jnp.max(scores, axis=1, keepdims=True)
    weights = jnp.exp(scores - top)
    denom = jnp.sum(weights, axis=1, keepdims=True)
    inverse = 1.0 / denom
    low = weights.astype(jnp.bfloat16)
    for window in range(WINDOWS):
        span = slice(window * WIN, (window + 1) * WIN)
        first = 3 * window * TREE
        numer = dot_n(low[first : first + SLOTS * TREE], value[:, span])
        part_ref[:, span] = own_lanes(numer * inverse[first : first + SLOTS * TREE], window)
    part_ref[:, width:] = heads_to_lanes(top + jnp.log(denom))

    leaf = jnp.where(
        lax.broadcasted_iota(jnp.int32, (LOW, TREE), 1) == info[0], 1.0, 0.0
    ).astype(jnp.bfloat16)
    chosen = dot_n(leaf, steps.astype(jnp.bfloat16))
    earlier = jnp.where(node_row <= node_col, 1.0, 0.0).astype(jnp.bfloat16)
    rank = dot_n(chosen.astype(jnp.bfloat16), earlier) - 1.0
    wanted = lax.broadcasted_iota(jnp.int32, (LOW, TREE), 0).astype(jnp.float32)
    is_key = (chosen > 0.5) & (rank == wanted) & (wanted < DEPTH)
    is_value = (chosen > 0.5) & (rank == wanted - DEPTH) & (rank < DEPTH)
    send_ref[...] = (
        dot_n(jnp.where(is_key, 1.0, 0.0).astype(jnp.bfloat16), key)
        + dot_n(jnp.where(is_value, 1.0, 0.0).astype(jnp.bfloat16), value)
    ).astype(jnp.bfloat16)


def tree(info, qkv, parent_hot):
    width = qkv.shape[1] // 3
    return pl.pallas_call(
        tree_body,
        out_shape=(
            jax.ShapeDtypeStruct((TREE, width + SIDE), jnp.float32),
            jax.ShapeDtypeStruct((LOW, width), jnp.bfloat16),
        ),
        in_specs=[pl.BlockSpec(memory_space=pltpu.SMEM)]
        + [pl.BlockSpec(memory_space=pltpu.VMEM)] * 2,
        out_specs=(pl.BlockSpec(memory_space=pltpu.VMEM),) * 2,
        compiler_params=pltpu.CompilerParams(vmem_limit_bytes=12 * 1024 * 1024),
        cost_estimate=LIGHT,
        name="tree",
    )(info, qkv, parent_hot)


def mix_body(spots, info, part_ref, own_ref, tree_ref, *rest):
    count = 1 + max(buffer for buffer, _ in spots)
    buffers = rest[:count]
    mid_ref, normed_ref, weights, sems = rest[count:]
    blocks = part_ref.shape[0]
    width = tree_ref.shape[1]
    rows = width // len(spots)
    copies = []
    for index, (buffer, row) in enumerate(spots):
        first = pl.multiple_of(info[index] * rows, 16)
        copies.append(
            pltpu.make_async_copy(
                buffers[buffer].at[pl.ds(row, rows)],
                weights.at[pl.ds(first, rows)],
                sems.at[index],
            )
        )
    for copy in copies:
        copy.start()

    lane = lax.broadcasted_iota(jnp.int32, (TREE, SIDE), 1)
    logs = []
    for block in range(blocks):
        packed = part_ref[block, :, width:].astype(jnp.float32)
        logs.append(
            packed + (pltpu.roll(packed, SIDE - 32, 1) + pltpu.roll(packed, SIDE - 64, 1))
        )
    logs.append(own_ref[:, width:])
    largest = functools.reduce(jnp.maximum, logs)
    shares = [jnp.exp(one - largest) for one in logs]
    whole = functools.reduce(jnp.add, shares)
    spread_rows = []
    for share in shares:
        share = share / whole
        high = share.astype(jnp.bfloat16).astype(jnp.float32)
        spread_rows.append(
            jnp.where(
                lane < LOW, high, jnp.where(lane < 2 * LOW, share - high, 0.0)
            ).astype(jnp.bfloat16)
        )
    spread_rows = jnp.concatenate(spread_rows, axis=0)
    for window in range(WINDOWS):
        span = slice(window * WIN, (window + 1) * WIN)
        head = lax.broadcasted_iota(jnp.int32, (SIDE, WIN), 0)
        column = lax.broadcasted_iota(jnp.int32, (SIDE, WIN), 1) + window * WIN
        first = (head & (H - 1)) * HD
        expand = jnp.where(
            (head < 2 * LOW) & (column >= first) & (column < first + HD), 1.0, 0.0
        ).astype(jnp.bfloat16)
        spread = dot_n(spread_rows, expand)
        mixed = spread[blocks * TREE :] * own_ref[:, span]
        for block in range(blocks):
            mixed = mixed + spread[block * TREE : (block + 1) * TREE] * part_ref[
                block, :, span
            ].astype(jnp.float32)
        mid_ref[:, span] = mixed.astype(jnp.bfloat16)

    attended = mid_ref[...]
    for copy in copies:
        copy.wait()
    proj = dot_t(attended, weights[...]).astype(jnp.bfloat16)
    mid = (tree_ref[...].astype(jnp.float32) + proj.astype(jnp.float32)).astype(jnp.bfloat16)
    mid_ref[...] = mid
    normed_ref[...] = rms_rows(mid)


def mix(info, parts, own, tree_input, buffers, spots):
    width = tree_input.shape[1]
    return pl.pallas_call(
        functools.partial(mix_body, spots),
        out_shape=(jax.ShapeDtypeStruct((TREE, width), jnp.bfloat16),) * 2,
        in_specs=[pl.BlockSpec(memory_space=pltpu.SMEM)]
        + [pl.BlockSpec(memory_space=pltpu.VMEM)] * 3
        + [HBM] * len(buffers),
        out_specs=(pl.BlockSpec(memory_space=pltpu.VMEM),) * 2,
        scratch_shapes=[
            pltpu.VMEM((width, width), jnp.bfloat16),
            pltpu.SemaphoreType.DMA((len(spots),)),
        ],
        compiler_params=pltpu.CompilerParams(vmem_limit_bytes=40 * 1024 * 1024),
        cost_estimate=LIGHT,
        name="mix",
    )(info, parts, own, tree_input, *buffers)


def feed_body(count, normed_ref, *rest):
    buffers, out_ref = rest[:count], rest[count]
    half = buffers[0].shape[0] // 2
    up = jnp.concatenate([buffer[:half] for buffer in buffers], axis=0)
    down = jnp.concatenate([buffer[half:] for buffer in buffers], axis=0)
    hidden = jax.nn.gelu(dot_t(normed_ref[...], up)).astype(jnp.bfloat16)
    out_ref[...] = dot_n(hidden, down).astype(out_ref.dtype)


def feed(normed, buffers, kind):
    return pl.pallas_call(
        functools.partial(feed_body, len(buffers)),
        out_shape=jax.ShapeDtypeStruct(normed.shape, kind),
        in_specs=[pl.BlockSpec(memory_space=pltpu.VMEM)] * (1 + len(buffers)),
        out_specs=pl.BlockSpec(memory_space=pltpu.VMEM),
        compiler_params=pltpu.CompilerParams(vmem_limit_bytes=24 * 1024 * 1024),
        cost_estimate=LIGHT,
        name="feed",
    )(normed, *buffers)


def finish_body(mid_ref, *rest):
    *parts, layer_ref, normed_ref = rest
    total = mid_ref[...].astype(jnp.float32)
    total = total + functools.reduce(
        jnp.add, [part[...].astype(jnp.float32) for part in parts]
    )
    layer = total.astype(jnp.bfloat16)
    layer_ref[...] = layer
    normed_ref[...] = rms_rows(layer)


def finish(mid, parts):
    return pl.pallas_call(
        finish_body,
        out_shape=(jax.ShapeDtypeStruct(mid.shape, jnp.bfloat16),) * 2,
        in_specs=[pl.BlockSpec(memory_space=pltpu.VMEM)] * (1 + len(parts)),
        out_specs=(pl.BlockSpec(memory_space=pltpu.VMEM),) * 2,
        cost_estimate=LIGHT,
        name="finish",
    )(mid, *parts)


def draft_body(rows_ref, w_ref, branch_ref):
    blocks = rows_ref.shape[0]
    rows = rows_ref[...].reshape(-1, rows_ref.shape[2])
    grown = jax.nn.silu(dot_t(rows, w_ref[...])).astype(jnp.bfloat16)
    for block in range(blocks):
        branch_ref[block] = grown[block * TREE : (block + 1) * TREE]


def draft(rows, w_draft_rows):
    blocks = rows.shape[0]
    columns, width = w_draft_rows.shape
    return pl.pallas_call(
        draft_body,
        out_shape=jax.ShapeDtypeStruct((blocks, TREE, columns), jnp.bfloat16),
        in_specs=[pl.BlockSpec(memory_space=pltpu.VMEM)] * 2,
        out_specs=pl.BlockSpec(memory_space=pltpu.VMEM),
        compiler_params=pltpu.CompilerParams(vmem_limit_bytes=12 * 1024 * 1024),
        cost_estimate=LIGHT,
        name="draft",
    )(rows, w_draft_rows)


def patch_body(heads, count, info, branch_ref, layer_ref, *rest):
    buffers = rest[:count]
    out_ref, weights, sems = rest[count:]
    blocks, _, columns = branch_ref.shape
    piece = columns // heads
    copies = []
    for index, buffer in enumerate(buffers):
        rows = buffer.shape[0]
        first = pl.multiple_of(info[index] * rows, 16)
        copies.append(
            pltpu.make_async_copy(buffer, weights.at[pl.ds(first, rows)], sems.at[index])
        )
    for copy in copies:
        copy.start()
    layer = layer_ref[...].astype(jnp.float32)
    drafted = []
    for head in range(heads):
        branch = jnp.concatenate(
            [
                branch_ref[block, :, head * piece : (head + 1) * piece].astype(jnp.float32)
                for block in range(blocks)
            ],
            axis=1,
        )
        drafted.append((layer + branch).astype(jnp.bfloat16))
    for copy in copies:
        copy.wait()
    product = dot_t(jnp.concatenate(drafted, axis=0), weights[...]).astype(jnp.bfloat16)
    for head in range(heads):
        out_ref[head] = product[head * TREE : (head + 1) * TREE]


def patch(info, branches, layer_out, buffers, heads):
    count = len(buffers)
    width = layer_out.shape[1]
    outputs = sum(buffer.shape[0] for buffer in buffers)
    return pl.pallas_call(
        functools.partial(patch_body, heads, count),
        out_shape=jax.ShapeDtypeStruct((heads, TREE, outputs), jnp.bfloat16),
        in_specs=[pl.BlockSpec(memory_space=pltpu.SMEM)]
        + [pl.BlockSpec(memory_space=pltpu.VMEM)] * 2
        + [HBM] * count,
        out_specs=pl.BlockSpec(memory_space=pltpu.VMEM),
        scratch_shapes=[
            pltpu.VMEM((outputs, width), jnp.bfloat16),
            pltpu.SemaphoreType.DMA((count,)),
        ],
        compiler_params=pltpu.CompilerParams(vmem_limit_bytes=16 * 1024 * 1024),
        cost_estimate=LIGHT,
        name="patch",
    )(info, branches, layer_out, *buffers)


def append_body(requests, count, info, *rest):
    sent = rest[:count]
    _, cache_ref, rows, blocks, load_sem, save_sem = rest[count:]

    def where(index, side):
        return cache_ref.at[side, pl.ds(pl.multiple_of(info[index], LOW), LOW)]

    def load(index, side):
        return pltpu.make_async_copy(
            where(index, side), blocks.at[index, side], load_sem.at[index, side]
        )

    def save(index, side):
        return pltpu.make_async_copy(
            blocks.at[index, side], where(index, side), save_sem.at[index, side]
        )

    def fetch(index, carry):
        @pl.when(info[index] >= 0)
        def _():
            for side in range(2):
                load(index, side).start()

        return carry

    def merge(index, carry):
        entry = index // 2
        request = info[5 * requests + entry]
        index = 2 * request + index % 2

        @pl.when(info[index] >= 0)
        def _():
            fresh = rows[entry].astype(jnp.float32)
            step = (
                lax.broadcasted_iota(jnp.int32, (LOW, fresh.shape[1]), 0)
                + info[2 * requests + index]
            )
            count = info[4 * requests + request]
            for side in range(2):
                load(index, side).wait()
                merged = blocks[index, side].astype(jnp.float32)
                for a in range(DEPTH):
                    row = fresh[side * DEPTH + a : side * DEPTH + a + 1]
                    merged = jnp.where((step == a) & (a < count), row, merged)
                blocks[index, side] = merged.astype(jnp.bfloat16)
                save(index, side).start()

        return carry

    def settle(index, carry):
        @pl.when(info[index] >= 0)
        def _():
            for side in range(2):
                save(index, side).wait()

        return carry

    lax.fori_loop(0, 2 * requests, fetch, 0)
    each = requests // count
    for index in range(count):
        for entry in range(each):
            rows[index * each + entry] = sent[index][entry * LOW : (entry + 1) * LOW]
    lax.fori_loop(0, 2 * requests, merge, 0)
    lax.fori_loop(0, 2 * requests, settle, 0)


def append(info, sent, cache, requests):
    width = cache.shape[2]
    count = len(sent)
    return pl.pallas_call(
        functools.partial(append_body, requests, count),
        out_shape=jax.ShapeDtypeStruct(cache.shape, cache.dtype),
        in_specs=[pl.BlockSpec(memory_space=pltpu.SMEM)]
        + [pl.BlockSpec(memory_space=pltpu.VMEM)] * count
        + [HBM],
        out_specs=HBM,
        input_output_aliases={1 + count: 0},
        scratch_shapes=[
            pltpu.VMEM((requests, LOW, width), jnp.bfloat16),
            pltpu.VMEM((2 * requests, 2, LOW, width), jnp.bfloat16),
            pltpu.SemaphoreType.DMA((2 * requests, 2)),
            pltpu.SemaphoreType.DMA((2 * requests, 2)),
        ],
        compiler_params=pltpu.CompilerParams(vmem_limit_bytes=24 * 1024 * 1024),
        cost_estimate=LIGHT,
        name="append",
    )(info, *sent, cache)


def after(values, earlier):
    return lax.optimization_barrier((values, earlier))[0]


def to_chips(shard):
    if lax.axis_size("blk") != 8:
        return [lax.all_gather(shard, "blk", axis=0, tiled=True)]
    return [shard] + [swap(shard, "blk", bits) for bits in (2, 4, 6)]


def to_cores(shards):
    if lax.axis_size("blk") != 8:
        return shards
    return shards + [swap(shard, "blk", 1) for shard in shards]


def pass_on(values, axis):
    size = lax.axis_size(axis)
    return lax.ppermute(values, axis, [(i, (i + 1) % size) for i in range(size)])


def swap(values, axis, bits):
    size = lax.axis_size(axis)
    return lax.ppermute(values, axis, [(i, i ^ bits) for i in range(size)])


def on_device(
    tree_input,
    cache,
    page_table,
    lengths,
    parents,
    accept_leaf,
    w_qkv,
    w_out,
    w_up,
    w_down,
    w_draft,
    w_patch,
):
    blocks = lax.axis_size("blk")
    myself = lax.axis_index("blk")
    lines = lax.axis_size("req")
    my_line = lax.axis_index("req")
    width = tree_input.shape[1]
    requests = lengths.shape[1]
    pool_pages = cache.shape[2] // PAGE
    heads = w_draft.shape[0]
    int32 = jnp.int32

    tree_all = lax.all_gather(tree_input, "blk", axis=0, tiled=True)
    projected = project(tree_all, w_qkv.T)
    out_rows = w_out.T
    feed_rows = jnp.concatenate([w_up.T, w_down])
    if blocks == 8:
        out_y = swap(after(out_rows, projected), "blk", 4)
    ring = [after(w_patch.T, projected)]
    ring.append(pass_on(ring[-1], "req"))
    projected = lax.all_to_all(projected, "blk", split_axis=0, concat_axis=0, tiled=True)
    projected = projected.transpose(1, 0, 2).reshape(tree_input.shape[0], -1)
    query_all = lax.all_gather(projected[:, :width], "blk", axis=0, tiled=True)
    if blocks == 8:
        query_all, out_y = lax.optimization_barrier((query_all, out_y))
        out_x = swap(jnp.concatenate([out_rows, out_y]), "blk", 2)
        feed_y = swap(after(feed_rows, query_all), "blk", 4)

    page_row, length_row, leaf_row = page_table[0], lengths[0], accept_leaf[0]
    total_pages = page_row.shape[0]
    npages = (length_row + DEPTH + PAGE - 1) // PAGE
    each = jnp.arange(requests, dtype=int32)
    page_ends = jnp.sum(
        jnp.where(each[None, :] <= each[:, None], npages[None, :], 0), axis=1
    )
    offsets = page_ends - npages
    local = jnp.arange(pool_pages, dtype=int32)
    places = jnp.arange(total_pages, dtype=int32)
    where_at = jnp.sum(
        jnp.where(page_row[None, :] == (myself * pool_pages + local)[:, None], places[None, :], 0),
        axis=1,
    )
    owner_hot = (offsets[None, :] <= where_at[:, None]) & (page_ends[None, :] > where_at[:, None])
    left = jnp.where(
        owner_hot, length_row[None, :] - (where_at[:, None] - offsets[None, :]) * PAGE, 0
    )
    limit = jnp.clip(jnp.sum(left, axis=1), 0, PAGE)
    used = limit > 0
    ranking = jnp.where(used, where_at, total_pages + local)
    rank = jnp.sum((ranking[None, :] < ranking[:, None]).astype(int32), axis=1)
    put = rank[None, :] == local[:, None]
    order = jnp.sum(jnp.where(put, local[None, :], 0), axis=1)
    limit_at = jnp.sum(jnp.where(put, limit[None, :], 0), axis=1)
    holds = (owner_hot & used[:, None]).astype(int32)
    count = jnp.sum(holds, axis=0)
    begin = jnp.sum(jnp.where(each[None, :] < each[:, None], count[None, :], 0), axis=1)
    page_info = jnp.concatenate([order, limit_at, begin, count])

    parts, cache_copy = attend(page_info, query_all, cache[0], requests)
    ring.append(pass_on(after(ring[-1], parts), "req"))
    projected = after(projected, parts)
    parts = lax.all_to_all(parts, "blk", split_axis=0, concat_axis=0, tiled=True)

    nodes = jnp.arange(TREE, dtype=int32)
    parent_hot = (parents[0][:, None] == nodes[None, :]).astype(jnp.float32)
    my_leaf = jnp.sum(jnp.where(each == myself, leaf_row, 0))
    own, sent = tree(my_leaf.astype(int32).reshape(1), projected, parent_hot)
    if blocks == 8:
        buffers = [out_rows, *after((out_y, out_x), own)]
        buffers += [swap(buffer, "blk", 1) for buffer in buffers]
        spots = ((0, 0), (1, 0), (2, 0), (2, out_rows.shape[0]))
        spots += tuple((buffer + 3, row) for buffer, row in spots)
        shards_at = [myself ^ bits for bits in (0, 4, 2, 6, 1, 5, 3, 7)]
        feeds = [feed_rows, after(feed_y, own)]
        feeds += [swap(buffer, "blk", 1) for buffer in feeds]
    else:
        buffers = [lax.all_gather(out_rows, "blk", axis=0, tiled=True)]
        spots = ((0, 0),)
        shards_at = [jnp.zeros((), int32)]
        halves = [lax.all_gather(one, "blk", axis=0, tiled=True) for one in (w_up.T, w_down)]
        feeds = [jnp.concatenate(halves)]
    mid, mid_normed = mix(
        jnp.stack([at.astype(int32) for at in shards_at]), parts, own, tree_input, buffers, spots
    )
    if blocks == 8:
        other = swap(mid_normed, "blk", 2)
        sums = [feed(mid_normed, feeds, jnp.float32)]
        sums.append(swap(feed(other, feeds, jnp.bfloat16), "blk", 2))
    else:
        sums = [feed(mid_normed, feeds, jnp.float32)]
    layer_out, draft_rows = finish(mid, sums)
    ring.append(pass_on(after(ring[-1], layer_out), "req"))
    if blocks == 8:
        draft_rows, *sent_near = lax.optimization_barrier((draft_rows, *to_chips(sent)))
    rows_all = lax.all_gather(draft_rows, "blk", axis=0, tiled=False)

    branch = draft(rows_all, w_draft.transpose(0, 2, 1).reshape(-1, width))
    branch = lax.all_to_all(branch, "blk", split_axis=0, concat_axis=0, tiled=True)
    patch_info = jnp.stack([(my_line + lines - step) % lines for step in range(lines)])
    drafts = patch(patch_info.astype(int32), branch, layer_out, ring, heads)

    if blocks == 8:
        sent_all = to_cores(sent_near)
        sent_by = myself ^ jnp.asarray(SHARDS_AT, int32)
    else:
        sent_all = [lax.all_gather(sent, "blk", axis=0, tiled=True)]
        sent_by = each
    level_marks = jnp.asarray(LEVEL_START[1:-1], int32)
    accepted = 1 + jnp.sum((leaf_row[:, None] >= level_marks[None, :]).astype(int32), axis=1)
    block_at = (length_row // LOW * LOW)[:, None] + jnp.arange(2, dtype=int32)[None, :] * LOW
    slot = jnp.minimum(offsets[:, None] + block_at // PAGE, total_pages - 1)
    page = jnp.sum(
        jnp.where(slot[:, :, None] == places[None, None, :], page_row[None, None, :], 0), axis=2
    )
    needed = (length_row + accepted)[:, None] > block_at
    row = jnp.where(
        needed & (page // pool_pages == myself),
        page % pool_pages * PAGE + block_at % PAGE,
        -1,
    )
    shift = block_at - length_row[:, None]
    append_info = jnp.concatenate([row.reshape(-1), shift.reshape(-1), accepted, sent_by])
    cache_new = append(append_info, sent_all, cache_copy, requests)[None]
    return (layer_out, drafts, cache_new)


def solution(mesh):
    in_specs = (
        P(("req", "blk"), None),
        P("req", None, "blk", None),
        P("req", None),
        P("req", None),
        P(("req", "blk"), None),
        P("req", None),
        P(None, "blk"),
        P(None, "blk"),
        P(None, "blk"),
        P("blk", None),
        P(None, None, "blk"),
        P(None, "req"),
    )
    out_specs = (
        P(("req", "blk"), None),
        P(None, ("req", "blk"), None),
        P("req", None, "blk", None),
    )
    return jax.shard_map(
        on_device, mesh=mesh, in_specs=in_specs, out_specs=out_specs, check_vma=False
    )
```

```python
import functools
import math

import jax
import jax.numpy as jnp
from jax import lax
from jax.experimental import pallas as pl
from jax.experimental.pallas import tpu as pltpu
from jax.sharding import PartitionSpec as P

H = 16
HD = 80
TREE = 48
DEPTH = 5
PAGE = 128
EPS = 1e-06
NEG = -1e30
LEVEL_START = (0, 1, 5, 15, 30, 48)
SCALE = 1.0 / math.sqrt(HD)

WIN = 256
WINDOWS = H * HD // WIN
SLOTS = 4
LOW = 16
SIDE = 128
LIGHT = pl.CostEstimate(flops=0, bytes_accessed=0, transcendentals=0)
HBM = pl.BlockSpec(memory_space=pltpu.HBM)


def rms_rows(values):
    wide = values.astype(jnp.float32)
    return (wide * lax.rsqrt(jnp.mean(wide * wide, axis=-1, keepdims=True) + EPS)).astype(
        jnp.bfloat16
    )


def dot_t(left, right):
    return lax.dot_general(
        left, right, (((1,), (1,)), ((), ())), preferred_element_type=jnp.float32
    )


def dot_n(left, right):
    return lax.dot_general(
        left, right, (((1,), (0,)), ((), ())), preferred_element_type=jnp.float32
    )


def in_head(window, slot, rows):
    lane = lax.broadcasted_iota(jnp.int32, (rows, WIN), 1)
    first = (3 * window + slot) * HD - window * WIN
    return (lane >= first) & (lane < first + HD)


def masked_queries(rows, window):
    part = rows[:, window * WIN : (window + 1) * WIN].astype(jnp.float32)
    slots = [
        jnp.where(in_head(window, slot, TREE), part, 0.0).astype(jnp.bfloat16)
        for slot in range(SLOTS)
    ]
    return jnp.concatenate(slots, axis=0)


def by_head(products):
    pieces = [None] * H
    for window, product in enumerate(products):
        for slot in range(SLOTS):
            piece = product[slot * TREE : (slot + 1) * TREE]
            head = 3 * window + slot
            pieces[head] = piece if pieces[head] is None else pieces[head] + piece
    return pieces


def own_lanes(product, window):
    total = None
    for slot in range(SLOTS):
        piece = jnp.where(
            in_head(window, slot, TREE), product[slot * TREE : (slot + 1) * TREE], 0.0
        )
        total = piece if total is None else total + piece
    return total


def heads_to_lanes(column):
    lane = lax.broadcasted_iota(jnp.int32, (TREE, SIDE), 1) & (H - 1)
    total = jnp.zeros((TREE, SIDE), jnp.float32)
    for head in range(H):
        total = jnp.where(lane == head, column[head * TREE : (head + 1) * TREE], total)
    return total


def three_parts(wide):
    lane = lax.broadcasted_iota(jnp.int32, wide.shape, 1)
    high = wide.astype(jnp.bfloat16).astype(jnp.float32)
    rest = wide - high
    middle = rest.astype(jnp.bfloat16).astype(jnp.float32)
    low = rest - middle
    return jnp.where(
        lane < 32, high, jnp.where(lane < 64, middle, jnp.where(lane < 96, low, 0.0))
    ).astype(jnp.bfloat16)


def attend_body(
    pages,
    requests,
    info,
    q_ref,
    cache_ref,
    part_ref,
    copy_ref,
    held,
    scores,
    queries,
    top,
    total,
    numer,
    load_sem,
    save_sem,
):
    width = q_ref.shape[1]

    def place(page):
        return pl.ds(pl.multiple_of(info[page] * PAGE, PAGE), PAGE)

    def load(side, page):
        return pltpu.make_async_copy(
            cache_ref.at[side, place(page)], held.at[side, page], load_sem.at[side, page]
        )

    def save(side, page):
        return pltpu.make_async_copy(
            held.at[side, page], copy_ref.at[side, place(page)], save_sem.at[side, page]
        )

    for side in range(2):
        for page in range(pages):
            load(side, page).start()

    def request(r, carry):
        begin = info[2 * pages + r]
        count = info[2 * pages + requests + r]

        @pl.when(count == 0)
        def _():
            part_ref[r, :, :width] = jnp.zeros((TREE, width), jnp.bfloat16)
            part_ref[r, :, width:] = three_parts(jnp.full((TREE, SIDE), NEG, jnp.float32))

        @pl.when(count > 0)
        def _():
            rows = q_ref[pl.ds(pl.multiple_of(r * TREE, 16), TREE), :]
            for window in range(WINDOWS):
                queries[window] = masked_queries(rows, window)
            top[...] = jnp.full(top.shape, NEG, jnp.float32)

            def score(i, carry):
                page = begin + i
                load(0, page).wait()
                save(0, page).start()
                keep = lax.broadcasted_iota(jnp.int32, (TREE, PAGE), 1) < info[pages + page]
                products = [
                    dot_t(
                        queries[window], held[0, page, :, window * WIN : (window + 1) * WIN]
                    )
                    for window in range(WINDOWS)
                ]
                for head, piece in enumerate(by_head(products)):
                    span = pl.ds(head * TREE, TREE)
                    masked = jnp.where(keep, piece * SCALE, NEG)
                    scores[page, span] = masked
                    top[span] = jnp.maximum(top[span], masked)
                return carry

            lax.fori_loop(0, count, score, 0)
            largest = jnp.max(top[...], axis=1, keepdims=True)
            top[...] = jnp.broadcast_to(largest, top.shape)
            total[...] = jnp.zeros(total.shape, jnp.float32)
            numer[...] = jnp.zeros(numer.shape, jnp.float32)

            def weigh(i, carry):
                page = begin + i
                load(1, page).wait()
                save(1, page).start()
                weights = jnp.exp(scores[page] - top[...])
                total[...] += weights
                low = weights.astype(jnp.bfloat16)
                for window in range(WINDOWS):
                    first = 3 * window * TREE
                    numer[window] += dot_n(
                        low[first : first + SLOTS * TREE],
                        held[1, page, :, window * WIN : (window + 1) * WIN],
                    )
                return carry

            lax.fori_loop(0, count, weigh, 0)
            denom = jnp.sum(total[...], axis=1, keepdims=True)
            inverse = 1.0 / denom
            for window in range(WINDOWS):
                first = 3 * window * TREE
                scaled = numer[window] * inverse[first : first + SLOTS * TREE]
                part_ref[r, :, window * WIN : (window + 1) * WIN] = own_lanes(
                    scaled, window
                ).astype(jnp.bfloat16)
            part_ref[r, :, width:] = three_parts(
                heads_to_lanes(top[:, :1] + jnp.log(denom))
            )

        return carry

    lax.fori_loop(0, requests, request, 0)
    used = info[2 * pages + requests - 1] + info[2 * pages + 2 * requests - 1]

    def untouched(page, carry):
        for side in range(2):
            load(side, page).wait()
            save(side, page).start()
        return carry

    lax.fori_loop(used, pages, untouched, 0)

    def settle(page, carry):
        for side in range(2):
            save(side, page).wait()
        return carry

    lax.fori_loop(0, pages, settle, 0)


def attend(info, query_all, cache, requests):
    pages = cache.shape[1] // PAGE
    width = query_all.shape[1]
    return pl.pallas_call(
        functools.partial(attend_body, pages, requests),
        out_shape=(
            jax.ShapeDtypeStruct((requests, TREE, width + SIDE), jnp.bfloat16),
            jax.ShapeDtypeStruct(cache.shape, cache.dtype),
        ),
        in_specs=[
            pl.BlockSpec(memory_space=pltpu.SMEM),
            pl.BlockSpec(memory_space=pltpu.VMEM),
            HBM,
        ],
        out_specs=(
            pl.BlockSpec(memory_space=pltpu.VMEM),
            HBM,
        ),
        scratch_shapes=[
            pltpu.VMEM((2, pages, PAGE, width), jnp.bfloat16),
            pltpu.VMEM((pages, H * TREE, PAGE), jnp.float32),
            pltpu.VMEM((WINDOWS, SLOTS * TREE, WIN), jnp.bfloat16),
            pltpu.VMEM((H * TREE, PAGE), jnp.float32),
            pltpu.VMEM((H * TREE, PAGE), jnp.float32),
            pltpu.VMEM((WINDOWS, SLOTS * TREE, WIN), jnp.float32),
            pltpu.SemaphoreType.DMA((2, pages)),
            pltpu.SemaphoreType.DMA((2, pages)),
        ],
        compiler_params=pltpu.CompilerParams(vmem_limit_bytes=52 * 1024 * 1024),
        cost_estimate=pl.CostEstimate(
            flops=4 * pages * PAGE * H * TREE * WIN,
            bytes_accessed=5 * cache.size,
            transcendentals=pages * PAGE * H * TREE,
        ),
        name="attend",
    )(info, query_all, cache)


def project_body(tree_ref, w_ref, out_ref):
    blocks = out_ref.shape[0]
    product = dot_t(rms_rows(tree_ref[...]), w_ref[...]).astype(jnp.bfloat16)
    for block in range(blocks):
        out_ref[block] = product[block * TREE : (block + 1) * TREE]


def project(tree_all, w_rows):
    rows, width = tree_all.shape
    columns = w_rows.shape[0]
    return pl.pallas_call(
        project_body,
        out_shape=jax.ShapeDtypeStruct((rows // TREE, TREE, columns), jnp.bfloat16),
        in_specs=[pl.BlockSpec(memory_space=pltpu.VMEM)] * 2,
        out_specs=pl.BlockSpec(memory_space=pltpu.VMEM),
        compiler_params=pltpu.CompilerParams(vmem_limit_bytes=24 * 1024 * 1024),
        cost_estimate=LIGHT,
        name="project",
    )(tree_all, w_rows)


def tree_body(info, qkv_ref, parent_ref, part_ref, send_ref):
    width = qkv_ref.shape[1] // 3
    node_row = lax.broadcasted_iota(jnp.int32, (TREE, TREE), 0)
    node_col = lax.broadcasted_iota(jnp.int32, (TREE, TREE), 1)
    steps = jnp.minimum(parent_ref[...] + jnp.where(node_row == node_col, 1.0, 0.0), 1.0)
    for _ in range(2):
        low = steps.astype(jnp.bfloat16)
        steps = jnp.minimum(dot_n(low, low), 1.0)
    marks = steps > 0.5

    query = qkv_ref[:, :width]
    key = qkv_ref[:, width : 2 * width]
    value = qkv_ref[:, 2 * width :]
    products = [
        dot_t(masked_queries(query, window), key[:, window * WIN : (window + 1) * WIN])
        for window in range(WINDOWS)
    ]
    scores = jnp.concatenate(
        [jnp.where(marks, piece * SCALE, NEG) for piece in by_head(products)], axis=0
    )
    top = jnp.max(scores, axis=1, keepdims=True)
    weights = jnp.exp(scores - top)
    denom = jnp.sum(weights, axis=1, keepdims=True)
    inverse = 1.0 / denom
    low = weights.astype(jnp.bfloat16)
    for window in range(WINDOWS):
        span = slice(window * WIN, (window + 1) * WIN)
        first = 3 * window * TREE
        numer = dot_n(low[first : first + SLOTS * TREE], value[:, span])
        part_ref[:, span] = own_lanes(numer * inverse[first : first + SLOTS * TREE], window)
    part_ref[:, width:] = heads_to_lanes(top + jnp.log(denom))

    leaf = jnp.where(
        lax.broadcasted_iota(jnp.int32, (LOW, TREE), 1) == info[0], 1.0, 0.0
    ).astype(jnp.bfloat16)
    chosen = dot_n(leaf, steps.astype(jnp.bfloat16))
    earlier = jnp.where(node_row <= node_col, 1.0, 0.0).astype(jnp.bfloat16)
    rank = dot_n(chosen.astype(jnp.bfloat16), earlier) - 1.0
    wanted = lax.broadcasted_iota(jnp.int32, (LOW, TREE), 0).astype(jnp.float32)
    is_key = (chosen > 0.5) & (rank == wanted) & (wanted < DEPTH)
    is_value = (chosen > 0.5) & (rank == wanted - DEPTH) & (rank < DEPTH)
    send_ref[...] = (
        dot_n(jnp.where(is_key, 1.0, 0.0).astype(jnp.bfloat16), key)
        + dot_n(jnp.where(is_value, 1.0, 0.0).astype(jnp.bfloat16), value)
    ).astype(jnp.bfloat16)


def tree(info, qkv, parent_hot):
    width = qkv.shape[1] // 3
    return pl.pallas_call(
        tree_body,
        out_shape=(
            jax.ShapeDtypeStruct((TREE, width + SIDE), jnp.float32),
            jax.ShapeDtypeStruct((LOW, width), jnp.bfloat16),
        ),
        in_specs=[pl.BlockSpec(memory_space=pltpu.SMEM)]
        + [pl.BlockSpec(memory_space=pltpu.VMEM)] * 2,
        out_specs=(pl.BlockSpec(memory_space=pltpu.VMEM),) * 2,
        compiler_params=pltpu.CompilerParams(vmem_limit_bytes=12 * 1024 * 1024),
        cost_estimate=LIGHT,
        name="tree",
    )(info, qkv, parent_hot)


def mix_body(count, info, part_ref, own_ref, tree_ref, sent_ref, *rest):
    buffers = rest[:count]
    mid_ref, normed_ref, weights, sems = rest[count:]
    blocks = part_ref.shape[0]
    width = tree_ref.shape[1]
    copies = []
    for index, buffer in enumerate(buffers):
        rows = buffer.shape[0]
        first = pl.multiple_of(info[index] * rows, 16)
        copies.append(
            pltpu.make_async_copy(buffer, weights.at[pl.ds(first, rows)], sems.at[index])
        )
    for copy in copies:
        copy.start()

    lane = lax.broadcasted_iota(jnp.int32, (TREE, SIDE), 1)
    logs = []
    for block in range(blocks):
        packed = part_ref[block, :, width:].astype(jnp.float32)
        logs.append(
            packed + (pltpu.roll(packed, SIDE - 32, 1) + pltpu.roll(packed, SIDE - 64, 1))
        )
    logs.append(own_ref[:, width:])
    largest = functools.reduce(jnp.maximum, logs)
    shares = [jnp.exp(one - largest) for one in logs]
    whole = functools.reduce(jnp.add, shares)
    spread_rows = []
    for share in shares:
        share = share / whole
        high = share.astype(jnp.bfloat16).astype(jnp.float32)
        spread_rows.append(
            jnp.where(
                lane < LOW, high, jnp.where(lane < 2 * LOW, share - high, 0.0)
            ).astype(jnp.bfloat16)
        )
    spread_rows = jnp.concatenate(spread_rows, axis=0)
    for window in range(WINDOWS):
        span = slice(window * WIN, (window + 1) * WIN)
        head = lax.broadcasted_iota(jnp.int32, (SIDE, WIN), 0)
        column = lax.broadcasted_iota(jnp.int32, (SIDE, WIN), 1) + window * WIN
        first = (head & (H - 1)) * HD
        expand = jnp.where(
            (head < 2 * LOW) & (column >= first) & (column < first + HD), 1.0, 0.0
        ).astype(jnp.bfloat16)
        spread = dot_n(spread_rows, expand)
        mixed = spread[blocks * TREE :] * own_ref[:, span]
        for block in range(blocks):
            mixed = mixed + spread[block * TREE : (block + 1) * TREE] * part_ref[
                block, :, span
            ].astype(jnp.float32)
        mid_ref[:, span] = mixed.astype(jnp.bfloat16)

    attended = mid_ref[...]
    for copy in copies:
        copy.wait()
    proj = dot_t(attended, weights[...]).astype(jnp.bfloat16)
    mid = (tree_ref[...].astype(jnp.float32) + proj.astype(jnp.float32)).astype(jnp.bfloat16)
    mid_ref[...] = mid
    normed_ref[:TREE] = rms_rows(mid)
    normed_ref[TREE:] = sent_ref[...]


def mix(info, parts, own, tree_input, sent, buffers):
    width = tree_input.shape[1]
    return pl.pallas_call(
        functools.partial(mix_body, len(buffers)),
        out_shape=(
            jax.ShapeDtypeStruct((TREE, width), jnp.bfloat16),
            jax.ShapeDtypeStruct((TREE + LOW, width), jnp.bfloat16),
        ),
        in_specs=[pl.BlockSpec(memory_space=pltpu.SMEM)]
        + [pl.BlockSpec(memory_space=pltpu.VMEM)] * 4
        + [HBM] * len(buffers),
        out_specs=(pl.BlockSpec(memory_space=pltpu.VMEM),) * 2,
        scratch_shapes=[
            pltpu.VMEM((width, width), jnp.bfloat16),
            pltpu.SemaphoreType.DMA((len(buffers),)),
        ],
        compiler_params=pltpu.CompilerParams(vmem_limit_bytes=60 * 1024 * 1024),
        cost_estimate=LIGHT,
        name="mix",
    )(info, parts, own, tree_input, sent, *buffers)


def feed_body(count, normed_ref, *rest):
    buffers, out_ref = rest[:count], rest[count]
    up = jnp.concatenate([buffer[: buffer.shape[0] // 2] for buffer in buffers], axis=0)
    down = jnp.concatenate([buffer[buffer.shape[0] // 2 :] for buffer in buffers], axis=0)
    hidden = jax.nn.gelu(dot_t(normed_ref[:TREE], up)).astype(jnp.bfloat16)
    out_ref[...] = dot_n(hidden, down).astype(out_ref.dtype)


def feed(normed, buffers, kind):
    return pl.pallas_call(
        functools.partial(feed_body, len(buffers)),
        out_shape=jax.ShapeDtypeStruct((TREE, normed.shape[1]), kind),
        in_specs=[pl.BlockSpec(memory_space=pltpu.VMEM)] * (1 + len(buffers)),
        out_specs=pl.BlockSpec(memory_space=pltpu.VMEM),
        compiler_params=pltpu.CompilerParams(vmem_limit_bytes=24 * 1024 * 1024),
        cost_estimate=LIGHT,
        name="feed",
    )(normed, *buffers)


def finish_body(mid_ref, *rest):
    *parts, layer_ref, normed_ref = rest
    total = mid_ref[...].astype(jnp.float32)
    total = total + functools.reduce(
        jnp.add, [part[...].astype(jnp.float32) for part in parts]
    )
    layer = total.astype(jnp.bfloat16)
    layer_ref[...] = layer
    normed_ref[...] = rms_rows(layer)


def finish(mid, parts):
    return pl.pallas_call(
        finish_body,
        out_shape=(jax.ShapeDtypeStruct(mid.shape, jnp.bfloat16),) * 2,
        in_specs=[pl.BlockSpec(memory_space=pltpu.VMEM)] * (1 + len(parts)),
        out_specs=(pl.BlockSpec(memory_space=pltpu.VMEM),) * 2,
        compiler_params=pltpu.CompilerParams(vmem_limit_bytes=8 * 1024 * 1024),
        cost_estimate=LIGHT,
        name="finish",
    )(mid, *parts)


def draft_body(rows_ref, w_ref, branch_ref):
    blocks = rows_ref.shape[0]
    rows = rows_ref[...].reshape(-1, rows_ref.shape[2])
    grown = jax.nn.silu(dot_t(rows, w_ref[...])).astype(jnp.bfloat16)
    for block in range(blocks):
        branch_ref[block] = grown[block * TREE : (block + 1) * TREE]


def draft(rows, w_draft_rows):
    blocks = rows.shape[0]
    columns, width = w_draft_rows.shape
    return pl.pallas_call(
        draft_body,
        out_shape=jax.ShapeDtypeStruct((blocks, TREE, columns), jnp.bfloat16),
        in_specs=[pl.BlockSpec(memory_space=pltpu.VMEM)] * 2,
        out_specs=pl.BlockSpec(memory_space=pltpu.VMEM),
        compiler_params=pltpu.CompilerParams(vmem_limit_bytes=12 * 1024 * 1024),
        cost_estimate=LIGHT,
        name="draft",
    )(rows, w_draft_rows)


def patch_body(heads, count, info, branch_ref, layer_ref, *rest):
    buffers = rest[:count]
    out_ref, weights, sems = rest[count:]
    blocks, _, columns = branch_ref.shape
    piece = columns // heads
    copies = []
    half = buffers[-1].shape[0]
    for index, buffer in enumerate(buffers):
        first = pl.multiple_of(info[index] * half, 16)
        copies.append(
            pltpu.make_async_copy(
                buffer, weights.at[pl.ds(first, buffer.shape[0])], sems.at[index]
            )
        )
    for copy in copies:
        copy.start()
    layer = layer_ref[...].astype(jnp.float32)
    drafted = []
    for head in range(heads):
        branch = jnp.concatenate(
            [
                branch_ref[block, :, head * piece : (head + 1) * piece].astype(jnp.float32)
                for block in range(blocks)
            ],
            axis=1,
        )
        drafted.append((layer + branch).astype(jnp.bfloat16))
    for copy in copies:
        copy.wait()
    product = dot_t(jnp.concatenate(drafted, axis=0), weights[...]).astype(jnp.bfloat16)
    for head in range(heads):
        out_ref[head] = product[head * TREE : (head + 1) * TREE]


def patch(info, branches, layer_out, buffers, heads):
    count = len(buffers)
    width = layer_out.shape[1]
    outputs = sum(buffer.shape[0] for buffer in buffers)
    return pl.pallas_call(
        functools.partial(patch_body, heads, count),
        out_shape=jax.ShapeDtypeStruct((heads, TREE, outputs), jnp.bfloat16),
        in_specs=[pl.BlockSpec(memory_space=pltpu.SMEM)]
        + [pl.BlockSpec(memory_space=pltpu.VMEM)] * 2
        + [HBM] * count,
        out_specs=pl.BlockSpec(memory_space=pltpu.VMEM),
        scratch_shapes=[
            pltpu.VMEM((outputs, width), jnp.bfloat16),
            pltpu.SemaphoreType.DMA((count,)),
        ],
        compiler_params=pltpu.CompilerParams(vmem_limit_bytes=16 * 1024 * 1024),
        cost_estimate=LIGHT,
        name="patch",
    )(info, branches, layer_out, *buffers)


def append_body(requests, count, info, *rest):
    sent = rest[:count]
    _, cache_ref, rows, blocks, load_sem, save_sem = rest[count:]

    def where(index, side):
        return cache_ref.at[side, pl.ds(pl.multiple_of(info[index], LOW), LOW)]

    def load(index, side):
        return pltpu.make_async_copy(
            where(index, side), blocks.at[index, side], load_sem.at[index, side]
        )

    def save(index, side):
        return pltpu.make_async_copy(
            blocks.at[index, side], where(index, side), save_sem.at[index, side]
        )

    def fetch(index, carry):
        @pl.when(info[index] >= 0)
        def _():
            for side in range(2):
                load(index, side).start()

        return carry

    def merge(index, carry):
        request = index // 2

        @pl.when(info[index] >= 0)
        def _():
            fresh = rows[pl.ds(pl.multiple_of(request * LOW, LOW), LOW)].astype(jnp.float32)
            step = (
                lax.broadcasted_iota(jnp.int32, (LOW, fresh.shape[1]), 0)
                + info[2 * requests + index]
            )
            count = info[4 * requests + request]
            for side in range(2):
                load(index, side).wait()
                merged = blocks[index, side].astype(jnp.float32)
                for a in range(DEPTH):
                    row = fresh[side * DEPTH + a : side * DEPTH + a + 1]
                    merged = jnp.where((step == a) & (a < count), row, merged)
                blocks[index, side] = merged.astype(jnp.bfloat16)
                save(index, side).start()

        return carry

    def settle(index, carry):
        @pl.when(info[index] >= 0)
        def _():
            for side in range(2):
                save(index, side).wait()

        return carry

    lax.fori_loop(0, 2 * requests, fetch, 0)
    entry = 0
    for buffer in sent:
        for first in range(0, buffer.shape[0], LOW):
            place = pl.multiple_of(info[5 * requests + entry] * LOW, LOW)
            rows[pl.ds(place, LOW)] = buffer[first : first + LOW]
            entry += 1
    lax.fori_loop(0, 2 * requests, merge, 0)
    lax.fori_loop(0, 2 * requests, settle, 0)


def append(info, sent, cache, requests):
    width = cache.shape[2]
    count = len(sent)
    return pl.pallas_call(
        functools.partial(append_body, requests, count),
        out_shape=jax.ShapeDtypeStruct(cache.shape, cache.dtype),
        in_specs=[pl.BlockSpec(memory_space=pltpu.SMEM)]
        + [pl.BlockSpec(memory_space=pltpu.VMEM)] * count
        + [HBM],
        out_specs=HBM,
        input_output_aliases={1 + count: 0},
        scratch_shapes=[
            pltpu.VMEM((requests * LOW, width), jnp.bfloat16),
            pltpu.VMEM((2 * requests, 2, LOW, width), jnp.bfloat16),
            pltpu.SemaphoreType.DMA((2 * requests, 2)),
            pltpu.SemaphoreType.DMA((2 * requests, 2)),
        ],
        compiler_params=pltpu.CompilerParams(vmem_limit_bytes=24 * 1024 * 1024),
        cost_estimate=LIGHT,
        name="append",
    )(info, *sent, cache)


def after(values, earlier):
    return lax.optimization_barrier((values, earlier))[0]


def pass_on(values, axis):
    size = lax.axis_size(axis)
    return lax.ppermute(values, axis, [(i, (i + 1) % size) for i in range(size)])


def swap(values, axis, bits):
    size = lax.axis_size(axis)
    return lax.ppermute(values, axis, [(i, i ^ bits) for i in range(size)])


def on_device(
    tree_input,
    cache,
    page_table,
    lengths,
    parents,
    accept_leaf,
    w_qkv,
    w_out,
    w_up,
    w_down,
    w_draft,
    w_patch,
):
    blocks = lax.axis_size("blk")
    myself = lax.axis_index("blk")
    lines = lax.axis_size("req")
    my_line = lax.axis_index("req")
    width = tree_input.shape[1]
    requests = lengths.shape[1]
    pool_pages = cache.shape[2] // PAGE
    heads = w_draft.shape[0]
    int32 = jnp.int32

    page_row, length_row, leaf_row = page_table[0], lengths[0], accept_leaf[0]
    total_pages = page_row.shape[0]
    npages = (length_row + DEPTH + PAGE - 1) // PAGE
    each = jnp.arange(requests, dtype=int32)
    page_ends = jnp.sum(
        jnp.where(each[None, :] <= each[:, None], npages[None, :], 0), axis=1
    )
    offsets = page_ends - npages
    local = jnp.arange(pool_pages, dtype=int32)
    places = jnp.arange(total_pages, dtype=int32)
    where_at = jnp.sum(
        jnp.where(page_row[None, :] == (myself * pool_pages + local)[:, None], places[None, :], 0),
        axis=1,
    )
    owner_hot = (offsets[None, :] <= where_at[:, None]) & (page_ends[None, :] > where_at[:, None])
    left = jnp.where(
        owner_hot, length_row[None, :] - (where_at[:, None] - offsets[None, :]) * PAGE, 0
    )
    limit = jnp.clip(jnp.sum(left, axis=1), 0, PAGE)
    used = limit > 0
    ranking = jnp.where(used, where_at, total_pages + local)
    rank = jnp.sum((ranking[None, :] < ranking[:, None]).astype(int32), axis=1)
    put = rank[None, :] == local[:, None]
    order = jnp.sum(jnp.where(put, local[None, :], 0), axis=1)
    limit_at = jnp.sum(jnp.where(put, limit[None, :], 0), axis=1)
    holds = (owner_hot & used[:, None]).astype(int32)
    count = jnp.sum(holds, axis=0)
    begin = jnp.sum(jnp.where(each[None, :] < each[:, None], count[None, :], 0), axis=1)
    page_info = jnp.concatenate([order, limit_at, begin, count])

    nodes = jnp.arange(TREE, dtype=int32)
    parent_hot = (parents[0][:, None] == nodes[None, :]).astype(jnp.float32)
    my_leaf = jnp.sum(jnp.where(each == myself, leaf_row, 0))
    leaf_info = my_leaf.astype(int32).reshape(1)
    if blocks == 8:
        mix_info = myself ^ jnp.asarray((0, 4, 2, 6, 1, 5, 3, 7), int32)
        sent_by = myself ^ jnp.asarray((0, 2, 4, 6, 1, 3, 5, 7), int32)
    else:
        mix_info = jnp.zeros((1,), int32)
        sent_by = each
    others = 2 * ((my_line + lines - jnp.arange(1, lines, dtype=int32)) % lines)
    patch_info = jnp.concatenate(
        [2 * my_line.reshape(1), others + myself % 2, others + (myself ^ 1) % 2]
    )
    level_marks = jnp.asarray(LEVEL_START[1:-1], int32)
    accepted = 1 + jnp.sum((leaf_row[:, None] >= level_marks[None, :]).astype(int32), axis=1)
    block_at = (length_row // LOW * LOW)[:, None] + jnp.arange(2, dtype=int32)[None, :] * LOW
    slot = jnp.minimum(offsets[:, None] + block_at // PAGE, total_pages - 1)
    page = jnp.sum(
        jnp.where(slot[:, :, None] == places[None, None, :], page_row[None, None, :], 0), axis=2
    )
    needed = (length_row + accepted)[:, None] > block_at
    row = jnp.where(
        needed & (page // pool_pages == myself),
        page % pool_pages * PAGE + block_at % PAGE,
        -1,
    )
    shift = block_at - length_row[:, None]
    append_info = jnp.concatenate([row.reshape(-1), shift.reshape(-1), accepted, sent_by])

    tree_all = lax.all_gather(tree_input, "blk", axis=0, tiled=True)
    projected = project(tree_all, w_qkv.T)
    out_rows = w_out.T
    feed_rows = jnp.concatenate([w_up.T, w_down])
    if blocks == 8:
        out_y = swap(after(out_rows, projected), "blk", 4)
        out_x = swap(after(out_rows, projected), "blk", 2)
        few = w_down.shape[0] // 2
        feed_half = jnp.concatenate(
            [
                lax.dynamic_slice_in_dim(one, my_line % 2 * few, few, 0)
                for one in (w_up.T, w_down)
            ]
        )
    half_rows = w_patch.shape[1] // 2
    my_half = lax.dynamic_slice_in_dim(w_patch.T, myself % 2 * half_rows, half_rows, 0)
    ring = [pass_on(after(my_half, projected), "req")]
    projected = lax.all_to_all(projected, "blk", split_axis=0, concat_axis=0, tiled=True)
    projected, page_info, append_info, leaf_info, mix_info, patch_info, parent_hot = (
        lax.optimization_barrier(
            (projected, page_info, append_info, leaf_info, mix_info, patch_info, parent_hot)
        )
    )
    projected = projected.transpose(1, 0, 2).reshape(tree_input.shape[0], -1)
    query_all = lax.all_gather(projected[:, :width], "blk", axis=0, tiled=True)
    query_all, ring[0] = lax.optimization_barrier((query_all, ring[0]))
    if blocks == 8:
        query_all, out_y, out_x = lax.optimization_barrier((query_all, out_y, out_x))
        out_xy = swap(out_y, "blk", 2)
        feed_y = swap(after(feed_half, query_all), "blk", 4)

    parts, cache_copy = attend(page_info, query_all, cache[0], requests)
    if blocks == 8:
        parts, out_xy, feed_y = lax.optimization_barrier((parts, out_xy, feed_y))
        feed_z = swap(feed_y, "req", 1)
        buffers = [out_rows, out_y, out_x, out_xy]
        buffers += [swap(buffer, "blk", 1) for buffer in after(tuple(buffers), parts)]
    else:
        buffers = [lax.all_gather(out_rows, "blk", axis=0, tiled=True)]
    projected, *buffers = lax.optimization_barrier((projected, *buffers))
    parts = lax.all_to_all(parts, "blk", split_axis=0, concat_axis=0, tiled=True)

    own, sent = tree(leaf_info, projected, parent_hot)
    ring.append(pass_on(after(ring[-1], own), "req"))
    parts, own = lax.optimization_barrier((parts, own))
    if blocks == 8:
        feeds = [feed_rows, *after((feed_y, feed_z), own)]
        feeds += [swap(buffer, "blk", 1) for buffer in feeds]
    else:
        halves = [lax.all_gather(one, "blk", axis=0, tiled=True) for one in (w_up.T, w_down)]
        feeds = [jnp.concatenate(halves)]
    mid, mid_normed = mix(mix_info, parts, own, tree_input, sent, buffers)
    mid, ring[-1] = lax.optimization_barrier((mid, ring[-1]))
    sums = [feed(mid_normed, feeds, jnp.float32)]
    if blocks == 8:
        other, sums[0] = lax.optimization_barrier((swap(mid_normed, "blk", 2), sums[0]))
        sent_all = [jnp.concatenate([sent, other[TREE:]])]
        other = feed(other, feeds, jnp.bfloat16)
        sent_all.append(swap(after(sent_all[0], other), "blk", 4))
        ring.append(pass_on(after(ring[-1], other), "req"))
        sums.append(swap(other, "blk", 2))
    else:
        ring.append(pass_on(after(ring[-1], sums[0]), "req"))
    layer_out, draft_rows = finish(mid, sums)
    rows_all = lax.all_gather(draft_rows, "blk", axis=0, tiled=False)
    if blocks == 8:
        rows_all, ring[-1], sent_all[-1] = lax.optimization_barrier(
            (rows_all, ring[-1], sent_all[-1])
        )
        sent_all += [swap(rows, "blk", 1) for rows in after(tuple(sent_all), rows_all)]
    else:
        sent_all = [lax.all_gather(sent, "blk", axis=0, tiled=True)]
    ring += [swap(after(half, rows_all), "blk", 1) for half in ring]

    branch = draft(rows_all, w_draft.transpose(0, 2, 1).reshape(-1, width))
    branch = lax.all_to_all(branch, "blk", split_axis=0, concat_axis=0, tiled=True)
    drafts = patch(patch_info, branch, layer_out, [w_patch.T, *ring], heads)

    cache_new = append(append_info, sent_all, cache_copy, requests)[None]
    return (layer_out, drafts, cache_new)


def solution(mesh):
    in_specs = (
        P(("req", "blk"), None),
        P("req", None, "blk", None),
        P("req", None),
        P("req", None),
        P(("req", "blk"), None),
        P("req", None),
        P(None, "blk"),
        P(None, "blk"),
        P(None, "blk"),
        P("blk", None),
        P(None, None, "blk"),
        P(None, "req"),
    )
    out_specs = (
        P(("req", "blk"), None),
        P(None, ("req", "blk"), None),
        P("req", None, "blk", None),
    )
    return jax.shard_map(
        on_device, mesh=mesh, in_specs=in_specs, out_specs=out_specs, check_vma=False
    )
```

```python
import functools
import math

import jax
import jax.numpy as jnp
from jax import lax
from jax.experimental import pallas as pl
from jax.experimental.pallas import tpu as pltpu
from jax.sharding import PartitionSpec as P

H = 16
HD = 80
TREE = 48
DEPTH = 5
PAGE = 128
EPS = 1e-06
NEG = -1e30
LEVEL_START = (0, 1, 5, 15, 30, 48)
SCALE = 1.0 / math.sqrt(HD)
EXPONENT = SCALE * math.log2(math.e)

WIN = 256
WINDOWS = H * HD // WIN
SLOTS = 4
LOW = 16
SIDE = 128
LIGHT = pl.CostEstimate(flops=0, bytes_accessed=0, transcendentals=0)
HBM = pl.BlockSpec(memory_space=pltpu.HBM)


def rms_rows(values):
    wide = values.astype(jnp.float32)
    return (wide * lax.rsqrt(jnp.mean(wide * wide, axis=-1, keepdims=True) + EPS)).astype(
        jnp.bfloat16
    )


def dot_t(left, right):
    return lax.dot_general(
        left, right, (((1,), (1,)), ((), ())), preferred_element_type=jnp.float32
    )


def dot_n(left, right):
    return lax.dot_general(
        left, right, (((1,), (0,)), ((), ())), preferred_element_type=jnp.float32
    )


def in_head(window, slot, rows):
    lane = lax.broadcasted_iota(jnp.int32, (rows, WIN), 1)
    first = (3 * window + slot) * HD - window * WIN
    return (lane >= first) & (lane < first + HD)


def masked_queries(rows, window):
    part = rows[:, window * WIN : (window + 1) * WIN].astype(jnp.float32)
    slots = [
        jnp.where(in_head(window, slot, TREE), part, 0.0).astype(jnp.bfloat16)
        for slot in range(SLOTS)
    ]
    return jnp.concatenate(slots, axis=0)


def by_head(products):
    pieces = [None] * H
    for window, product in enumerate(products):
        for slot in range(SLOTS):
            piece = product[slot * TREE : (slot + 1) * TREE]
            head = 3 * window + slot
            pieces[head] = piece if pieces[head] is None else pieces[head] + piece
    return pieces


def own_lanes(product, window):
    total = None
    for slot in range(SLOTS):
        piece = jnp.where(
            in_head(window, slot, TREE), product[slot * TREE : (slot + 1) * TREE], 0.0
        )
        total = piece if total is None else total + piece
    return total


def heads_to_lanes(column):
    lane = lax.broadcasted_iota(jnp.int32, (TREE, SIDE), 1) & (H - 1)
    total = jnp.zeros((TREE, SIDE), jnp.float32)
    for head in range(H):
        total = jnp.where(lane == head, column[head * TREE : (head + 1) * TREE], total)
    return total


def split_heads(shares):
    lane = lax.broadcasted_iota(jnp.int32, shares.shape, 1)
    high = shares.astype(jnp.bfloat16).astype(jnp.float32)
    split = jnp.where(lane < LOW, high, jnp.where(lane < 2 * LOW, shares - high, 0.0))
    return split.astype(jnp.bfloat16)


def head_columns(window):
    head = lax.broadcasted_iota(jnp.int32, (SIDE, WIN), 0)
    column = lax.broadcasted_iota(jnp.int32, (SIDE, WIN), 1) + window * WIN
    first = (head & (H - 1)) * HD
    return jnp.where(
        (head < 2 * LOW) & (column >= first) & (column < first + HD), 1.0, 0.0
    ).astype(jnp.bfloat16)


def three_parts(wide):
    lane = lax.broadcasted_iota(jnp.int32, wide.shape, 1)
    high = wide.astype(jnp.bfloat16).astype(jnp.float32)
    rest = wide - high
    middle = rest.astype(jnp.bfloat16).astype(jnp.float32)
    low = rest - middle
    return jnp.where(
        lane < 32, high, jnp.where(lane < 64, middle, jnp.where(lane < 96, low, 0.0))
    ).astype(jnp.bfloat16)


def attend_body(pages, requests, cores, info, q_ref, cache_ref, *rest):
    part_refs, copy_ref, *rest = rest[:cores], *rest[cores:]
    held, scores, queries, top, total, numer, expand, load_sem, save_sem = rest
    width = q_ref.shape[1]

    def place(page):
        return pl.ds(pl.multiple_of(info[page] * PAGE, PAGE), PAGE)

    def load(side, page):
        return pltpu.make_async_copy(
            cache_ref.at[side, place(page)], held.at[side, page], load_sem.at[side, page]
        )

    def save(side, page):
        return pltpu.make_async_copy(
            held.at[side, page], copy_ref.at[side, place(page)], save_sem.at[side, page]
        )

    core = info[2 * pages + 2 * requests]

    for side in range(2):
        for page in range(pages):
            load(side, page).start()
    for window in range(WINDOWS):
        expand[window] = head_columns(window)
    ones = jnp.ones((2 * SIDE, SIDE), jnp.bfloat16)

    def score(page, many, fresh):
        for one in range(many):
            load(0, page + one).wait()
            save(0, page + one).start()
        lane = lax.broadcasted_iota(jnp.int32, (TREE, PAGE), 1)
        products = []
        for window in range(WINDOWS):
            keys = held[0, pl.ds(page, many), :, window * WIN : (window + 1) * WIN]
            products.append(dot_t(queries[window], keys.reshape(many * PAGE, WIN)))
        keep = [lane < info[pages + page + one] for one in range(many)]
        for head, piece in enumerate(by_head(products)):
            span = pl.ds(head * TREE, TREE)
            largest = None if fresh else top[span]
            for one in range(many):
                masked = jnp.where(keep[one], piece[:, one * PAGE : (one + 1) * PAGE], NEG)
                scores[page + one, span] = masked
                largest = masked if largest is None else jnp.maximum(largest, masked)
            top[span] = largest

    def weigh(page, many, fresh):
        for one in range(many):
            load(1, page + one).wait()
            save(1, page + one).start()
        largest = top[...]
        weights = [
            jnp.exp2((scores[page + one] - largest) * EXPONENT) for one in range(many)
        ]
        added = functools.reduce(jnp.add, weights)
        total[...] = added if fresh else total[...] + added
        low = jnp.concatenate([one.astype(jnp.bfloat16) for one in weights], axis=1)
        for window in range(WINDOWS):
            first = 3 * window * TREE
            values = held[1, pl.ds(page, many), :, window * WIN : (window + 1) * WIN]
            product = dot_n(low[first : first + SLOTS * TREE], values.reshape(many * PAGE, WIN))
            numer[window] = product if fresh else numer[window] + product

    def over(step, begin, count):
        odd = count % 2

        @pl.when(odd == 1)
        def _():
            step(begin, 1, True)

        @pl.when(odd == 0)
        def _():
            step(begin, 2, True)

        def pair(i, carry):
            step(begin + 2 * i - odd, 2, False)
            return carry

        lax.fori_loop(1, (count + odd) // 2, pair, 0)

    def give(part):
        high = total[...].astype(jnp.bfloat16)
        rest = (total[...] - high.astype(jnp.float32)).astype(jnp.bfloat16)
        total[...] = dot_n(jnp.concatenate([high, rest], axis=1), ones)
        denom = heads_to_lanes(total)
        inverse = split_heads(1.0 / denom)
        for window in range(WINDOWS):
            part[:, window * WIN : (window + 1) * WIN] = (
                own_lanes(numer[window], window) * dot_n(inverse, expand[window])
            ).astype(jnp.bfloat16)
        part[:, width:] = three_parts(heads_to_lanes(top) * SCALE + jnp.log(denom))

    def give_none(part):
        part[:, :width] = jnp.zeros((TREE, width), jnp.bfloat16)
        part[:, width:] = three_parts(jnp.full((TREE, SIDE), NEG, jnp.float32))

    def to_output(r, act):
        for index, part_ref in enumerate(part_refs):

            @pl.when((r + core) % cores == index)
            def _():
                act(part_ref.at[r // cores])

    def request(r, carry):
        begin = info[2 * pages + r]
        count = info[2 * pages + requests + r]

        @pl.when(count == 0)
        def _():
            to_output(r, give_none)

        @pl.when(count > 0)
        def _():
            rows = q_ref[pl.ds(pl.multiple_of(r * TREE, 16), TREE), :]
            for window in range(WINDOWS):
                queries[window] = masked_queries(rows, window)
            over(score, begin, count)
            largest = jnp.max(top[...], axis=1, keepdims=True)
            top[...] = jnp.broadcast_to(largest, top.shape)
            over(weigh, begin, count)
            to_output(r, give)

        return carry

    lax.fori_loop(0, requests, request, 0)
    used = info[2 * pages + requests - 1] + info[2 * pages + 2 * requests - 1]

    def untouched(page, carry):
        for side in range(2):
            load(side, page).wait()
            save(side, page).start()
        return carry

    lax.fori_loop(used, pages, untouched, 0)

    def settle(page, carry):
        for side in range(2):
            save(side, page).wait()
        return carry

    lax.fori_loop(0, pages, settle, 0)


def attend(info, query_all, cache, requests, cores):
    pages = cache.shape[1] // PAGE
    width = query_all.shape[1]
    parts = jax.ShapeDtypeStruct((requests // cores, TREE, width + SIDE), jnp.bfloat16)
    return pl.pallas_call(
        functools.partial(attend_body, pages, requests, cores),
        out_shape=(parts,) * cores + (jax.ShapeDtypeStruct(cache.shape, cache.dtype),),
        in_specs=[
            pl.BlockSpec(memory_space=pltpu.SMEM),
            pl.BlockSpec(memory_space=pltpu.VMEM),
            HBM,
        ],
        out_specs=(pl.BlockSpec(memory_space=pltpu.VMEM),) * cores + (HBM,),
        scratch_shapes=[
            pltpu.VMEM((2, pages, PAGE, width), jnp.bfloat16),
            pltpu.VMEM((pages, H * TREE, PAGE), jnp.float32),
            pltpu.VMEM((WINDOWS, SLOTS * TREE, WIN), jnp.bfloat16),
            pltpu.VMEM((H * TREE, PAGE), jnp.float32),
            pltpu.VMEM((H * TREE, PAGE), jnp.float32),
            pltpu.VMEM((WINDOWS, SLOTS * TREE, WIN), jnp.float32),
            pltpu.VMEM((WINDOWS, SIDE, WIN), jnp.bfloat16),
            pltpu.SemaphoreType.DMA((2, pages)),
            pltpu.SemaphoreType.DMA((2, pages)),
        ],
        compiler_params=pltpu.CompilerParams(vmem_limit_bytes=51 * 1024 * 1024),
        cost_estimate=pl.CostEstimate(
            flops=4 * pages * PAGE * H * TREE * WIN,
            bytes_accessed=5 * cache.size,
            transcendentals=pages * PAGE * H * TREE,
        ),
        name="attend",
    )(info, query_all, cache)


def whole_log(packed):
    wide = packed.astype(jnp.float32)
    return wide + (pltpu.roll(wide, SIDE - 32, 1) + pltpu.roll(wide, SIDE - 64, 1))


def merge_body(kept_ref, got_ref, out_ref):
    chips = out_ref.shape[0]
    width = out_ref.shape[2] - SIDE
    lane = lax.broadcasted_iota(jnp.int32, (TREE, SIDE), 1)
    shares = []
    for chip in range(chips):
        logs = [whole_log(ref[chip, :, width:]) for ref in (kept_ref, got_ref)]
        largest = jnp.maximum(*logs)
        terms = [jnp.exp(one - largest) for one in logs]
        whole = terms[0] + terms[1]
        shares += [term / whole for term in terms]
        joined = jnp.where(lane < 32, largest + jnp.log(whole), 0.0)
        joined = joined + pltpu.roll(joined, 32, 1) + pltpu.roll(joined, 64, 1)
        out_ref[chip, :, width:] = three_parts(joined)
    shares = split_heads(jnp.concatenate(shares, axis=0))
    for window in range(WINDOWS):
        span = slice(window * WIN, (window + 1) * WIN)
        spread = dot_n(shares, head_columns(window))
        for chip in range(chips):
            total = 0.0
            for one, ref in enumerate((kept_ref, got_ref)):
                first = (2 * chip + one) * TREE
                total += spread[first : first + TREE] * ref[chip, :, span].astype(jnp.float32)
            out_ref[chip, :, span] = total.astype(jnp.bfloat16)


def merge(kept, got):
    return pl.pallas_call(
        merge_body,
        out_shape=jax.ShapeDtypeStruct(kept.shape, jnp.bfloat16),
        in_specs=[pl.BlockSpec(memory_space=pltpu.VMEM)] * 2,
        out_specs=pl.BlockSpec(memory_space=pltpu.VMEM),
        compiler_params=pltpu.CompilerParams(vmem_limit_bytes=16 * 1024 * 1024),
        cost_estimate=LIGHT,
        name="merge",
    )(kept, got)


def project_body(tree_ref, w_ref, out_ref):
    blocks = out_ref.shape[0]
    product = dot_t(rms_rows(tree_ref[...]), w_ref[...]).astype(jnp.bfloat16)
    for block in range(blocks):
        out_ref[block] = product[block * TREE : (block + 1) * TREE]


def project(tree_all, w_rows):
    rows, width = tree_all.shape
    columns = w_rows.shape[0]
    return pl.pallas_call(
        project_body,
        out_shape=jax.ShapeDtypeStruct((rows // TREE, TREE, columns), jnp.bfloat16),
        in_specs=[pl.BlockSpec(memory_space=pltpu.VMEM)] * 2,
        out_specs=pl.BlockSpec(memory_space=pltpu.VMEM),
        compiler_params=pltpu.CompilerParams(vmem_limit_bytes=24 * 1024 * 1024),
        cost_estimate=LIGHT,
        name="project",
    )(tree_all, w_rows)


def tree_body(info, qkv_ref, parent_ref, part_ref, send_ref):
    mine = info[info[info.shape[0] - 1]]
    width = qkv_ref.shape[1] // 3
    node_row = lax.broadcasted_iota(jnp.int32, (TREE, TREE), 0)
    node_col = lax.broadcasted_iota(jnp.int32, (TREE, TREE), 1)
    steps = jnp.minimum(parent_ref[...] + jnp.where(node_row == node_col, 1.0, 0.0), 1.0)
    for _ in range(2):
        low = steps.astype(jnp.bfloat16)
        steps = jnp.minimum(dot_n(low, low), 1.0)
    marks = steps > 0.5

    query = qkv_ref[:, :width]
    key = qkv_ref[:, width : 2 * width]
    value = qkv_ref[:, 2 * width :]
    products = [
        dot_t(masked_queries(query, window), key[:, window * WIN : (window + 1) * WIN])
        for window in range(WINDOWS)
    ]
    scores = jnp.concatenate(
        [jnp.where(marks, piece * SCALE, NEG) for piece in by_head(products)], axis=0
    )
    top = jnp.max(scores, axis=1, keepdims=True)
    weights = jnp.exp(scores - top)
    denom = jnp.sum(weights, axis=1, keepdims=True)
    inverse = 1.0 / denom
    low = weights.astype(jnp.bfloat16)
    for window in range(WINDOWS):
        span = slice(window * WIN, (window + 1) * WIN)
        first = 3 * window * TREE
        numer = dot_n(low[first : first + SLOTS * TREE], value[:, span])
        part_ref[:, span] = own_lanes(numer * inverse[first : first + SLOTS * TREE], window)
    part_ref[:, width:] = heads_to_lanes(top + jnp.log(denom))

    leaf = jnp.where(
        lax.broadcasted_iota(jnp.int32, (LOW, TREE), 1) == mine, 1.0, 0.0
    ).astype(jnp.bfloat16)
    chosen = dot_n(leaf, steps.astype(jnp.bfloat16))
    earlier = jnp.where(node_row <= node_col, 1.0, 0.0).astype(jnp.bfloat16)
    rank = dot_n(chosen.astype(jnp.bfloat16), earlier) - 1.0
    wanted = lax.broadcasted_iota(jnp.int32, (LOW, TREE), 0).astype(jnp.float32)
    is_key = (chosen > 0.5) & (rank == wanted) & (wanted < DEPTH)
    is_value = (chosen > 0.5) & (rank == wanted - DEPTH) & (rank < DEPTH)
    send_ref[...] = (
        dot_n(jnp.where(is_key, 1.0, 0.0).astype(jnp.bfloat16), key)
        + dot_n(jnp.where(is_value, 1.0, 0.0).astype(jnp.bfloat16), value)
    ).astype(jnp.bfloat16)


def tree(info, qkv, parent_hot):
    width = qkv.shape[1] // 3
    return pl.pallas_call(
        tree_body,
        out_shape=(
            jax.ShapeDtypeStruct((TREE, width + SIDE), jnp.float32),
            jax.ShapeDtypeStruct((LOW, width), jnp.bfloat16),
        ),
        in_specs=[pl.BlockSpec(memory_space=pltpu.SMEM)]
        + [pl.BlockSpec(memory_space=pltpu.VMEM)] * 2,
        out_specs=(pl.BlockSpec(memory_space=pltpu.VMEM),) * 2,
        compiler_params=pltpu.CompilerParams(vmem_limit_bytes=12 * 1024 * 1024),
        cost_estimate=LIGHT,
        name="tree",
    )(info, qkv, parent_hot)


def mix_body(count, info, part_ref, own_ref, tree_ref, sent_ref, *rest):
    parts = [part_ref.at[block] for block in range(part_ref.shape[0])]
    buffers = rest[:count]
    mid_ref, normed_ref, weights, sems = rest[count:]
    width = tree_ref.shape[1]
    copies = []
    for index, buffer in enumerate(buffers):
        rows = buffer.shape[0]
        first = pl.multiple_of(info[index] * rows, 16)
        copies.append(
            pltpu.make_async_copy(buffer, weights.at[pl.ds(first, rows)], sems.at[index])
        )
    for copy in copies:
        copy.start()

    logs = [whole_log(part[:, width:]) for part in parts] + [own_ref[:, width:]]
    largest = functools.reduce(jnp.maximum, logs)
    terms = [jnp.exp(one - largest) for one in logs]
    whole = functools.reduce(jnp.add, terms)
    shares = split_heads(jnp.concatenate([term / whole for term in terms], axis=0))
    for window in range(WINDOWS):
        span = slice(window * WIN, (window + 1) * WIN)
        spread = dot_n(shares, head_columns(window))
        mixed = spread[len(parts) * TREE :] * own_ref[:, span]
        for index, part in enumerate(parts):
            first = index * TREE
            mixed += spread[first : first + TREE] * part[:, span].astype(jnp.float32)
        mid_ref[:, span] = mixed.astype(jnp.bfloat16)

    attended = mid_ref[...]
    for copy in copies:
        copy.wait()
    proj = dot_t(attended, weights[...]).astype(jnp.bfloat16)
    mid = (tree_ref[...].astype(jnp.float32) + proj.astype(jnp.float32)).astype(jnp.bfloat16)
    mid_ref[...] = mid
    normed_ref[:TREE] = rms_rows(mid)
    normed_ref[TREE:] = sent_ref[...]


def mix(info, parts, own, tree_input, sent, buffers):
    width = tree_input.shape[1]
    return pl.pallas_call(
        functools.partial(mix_body, len(buffers)),
        out_shape=(
            jax.ShapeDtypeStruct((TREE, width), jnp.bfloat16),
            jax.ShapeDtypeStruct((TREE + LOW, width), jnp.bfloat16),
        ),
        in_specs=[pl.BlockSpec(memory_space=pltpu.SMEM)]
        + [pl.BlockSpec(memory_space=pltpu.VMEM)] * 4
        + [HBM] * len(buffers),
        out_specs=(pl.BlockSpec(memory_space=pltpu.VMEM),) * 2,
        scratch_shapes=[
            pltpu.VMEM((width, width), jnp.bfloat16),
            pltpu.SemaphoreType.DMA((len(buffers),)),
        ],
        compiler_params=pltpu.CompilerParams(vmem_limit_bytes=60 * 1024 * 1024),
        cost_estimate=LIGHT,
        name="mix",
    )(info, parts, own, tree_input, sent, *buffers)


def feed_body(count, normed_ref, *rest):
    buffers, out_ref = rest[:count], rest[count]
    half = buffers[0].shape[0] // 2
    up = jnp.concatenate([buffer[:half] for buffer in buffers], axis=0)
    down = jnp.concatenate([buffer[half:] for buffer in buffers], axis=0)
    hidden = jax.nn.gelu(dot_t(normed_ref[:TREE], up)).astype(jnp.bfloat16)
    out_ref[...] = dot_n(hidden, down).astype(out_ref.dtype)


def feed(normed, buffers, kind):
    return pl.pallas_call(
        functools.partial(feed_body, len(buffers)),
        out_shape=jax.ShapeDtypeStruct((TREE, normed.shape[1]), kind),
        in_specs=[pl.BlockSpec(memory_space=pltpu.VMEM)] * (1 + len(buffers)),
        out_specs=pl.BlockSpec(memory_space=pltpu.VMEM),
        compiler_params=pltpu.CompilerParams(vmem_limit_bytes=24 * 1024 * 1024),
        cost_estimate=LIGHT,
        name="feed",
    )(normed, *buffers)


def finish_body(mid_ref, *rest):
    *parts, layer_ref, normed_ref = rest
    total = mid_ref[...].astype(jnp.float32)
    total = total + functools.reduce(
        jnp.add, [part[...].astype(jnp.float32) for part in parts]
    )
    layer = total.astype(jnp.bfloat16)
    layer_ref[...] = layer
    normed_ref[...] = rms_rows(layer)


def finish(mid, parts):
    return pl.pallas_call(
        finish_body,
        out_shape=(jax.ShapeDtypeStruct(mid.shape, jnp.bfloat16),) * 2,
        in_specs=[pl.BlockSpec(memory_space=pltpu.VMEM)] * (1 + len(parts)),
        out_specs=(pl.BlockSpec(memory_space=pltpu.VMEM),) * 2,
        compiler_params=pltpu.CompilerParams(vmem_limit_bytes=8 * 1024 * 1024),
        cost_estimate=LIGHT,
        name="finish",
    )(mid, *parts)


def draft_body(rows_ref, w_ref, branch_ref):
    blocks = rows_ref.shape[0]
    rows = rows_ref[...].reshape(-1, rows_ref.shape[2])
    grown = jax.nn.silu(dot_t(rows, w_ref[...])).astype(jnp.bfloat16)
    for block in range(blocks):
        branch_ref[block] = grown[block * TREE : (block + 1) * TREE]


def draft(rows, w_draft_rows):
    blocks = rows.shape[0]
    columns, width = w_draft_rows.shape
    return pl.pallas_call(
        draft_body,
        out_shape=jax.ShapeDtypeStruct((blocks, TREE, columns), jnp.bfloat16),
        in_specs=[pl.BlockSpec(memory_space=pltpu.VMEM)] * 2,
        out_specs=pl.BlockSpec(memory_space=pltpu.VMEM),
        compiler_params=pltpu.CompilerParams(vmem_limit_bytes=12 * 1024 * 1024),
        cost_estimate=LIGHT,
        name="draft",
    )(rows, w_draft_rows)


def patch_body(heads, count, info, branch_ref, layer_ref, *rest):
    buffers = rest[:count]
    out_ref, weights = rest[count:]
    blocks, _, columns = branch_ref.shape
    piece = columns // heads
    half = buffers[-1].shape[0]
    for index, buffer in enumerate(buffers):
        first = pl.multiple_of(info[index] * half, 16)
        weights[pl.ds(first, buffer.shape[0])] = buffer[...]
    layer = layer_ref[...].astype(jnp.float32)
    drafted = []
    for head in range(heads):
        branch = jnp.concatenate(
            [
                branch_ref[block, :, head * piece : (head + 1) * piece].astype(jnp.float32)
                for block in range(blocks)
            ],
            axis=1,
        )
        drafted.append((layer + branch).astype(jnp.bfloat16))
    product = dot_t(jnp.concatenate(drafted, axis=0), weights[...]).astype(jnp.bfloat16)
    for head in range(heads):
        out_ref[head] = product[head * TREE : (head + 1) * TREE]


def patch(info, branches, layer_out, buffers, heads):
    count = len(buffers)
    width = layer_out.shape[1]
    outputs = sum(buffer.shape[0] for buffer in buffers)
    return pl.pallas_call(
        functools.partial(patch_body, heads, count),
        out_shape=jax.ShapeDtypeStruct((heads, TREE, outputs), jnp.bfloat16),
        in_specs=[pl.BlockSpec(memory_space=pltpu.SMEM)]
        + [pl.BlockSpec(memory_space=pltpu.VMEM)] * (2 + count),
        out_specs=pl.BlockSpec(memory_space=pltpu.VMEM),
        scratch_shapes=[pltpu.VMEM((outputs, width), jnp.bfloat16)],
        compiler_params=pltpu.CompilerParams(vmem_limit_bytes=24 * 1024 * 1024),
        cost_estimate=LIGHT,
        name="patch",
    )(info, branches, layer_out, *buffers)


def append_body(requests, count, info, *rest):
    sent = rest[:count]
    _, cache_ref, rows, blocks, load_sem, save_sem = rest[count:]

    def where(index, side):
        return cache_ref.at[side, pl.ds(pl.multiple_of(info[index], LOW), LOW)]

    def load(index, side):
        return pltpu.make_async_copy(
            where(index, side), blocks.at[index, side], load_sem.at[index, side]
        )

    def save(index, side):
        return pltpu.make_async_copy(
            blocks.at[index, side], where(index, side), save_sem.at[index, side]
        )

    def fetch(index, carry):
        @pl.when(info[index] >= 0)
        def _():
            for side in range(2):
                load(index, side).start()

        return carry

    def merge(index, carry):
        request = index // 2

        @pl.when(info[index] >= 0)
        def _():
            fresh = rows[pl.ds(pl.multiple_of(request * LOW, LOW), LOW)].astype(jnp.float32)
            step = (
                lax.broadcasted_iota(jnp.int32, (LOW, fresh.shape[1]), 0)
                + info[2 * requests + index]
            )
            count = info[4 * requests + request]
            for side in range(2):
                load(index, side).wait()
                merged = blocks[index, side].astype(jnp.float32)
                for a in range(DEPTH):
                    row = fresh[side * DEPTH + a : side * DEPTH + a + 1]
                    merged = jnp.where((step == a) & (a < count), row, merged)
                blocks[index, side] = merged.astype(jnp.bfloat16)
                save(index, side).start()

        return carry

    def settle(index, carry):
        @pl.when(info[index] >= 0)
        def _():
            for side in range(2):
                save(index, side).wait()

        return carry

    lax.fori_loop(0, 2 * requests, fetch, 0)
    entry = 0
    for buffer in sent:
        for first in range(0, buffer.shape[0], LOW):
            place = pl.multiple_of(info[5 * requests + entry] * LOW, LOW)
            rows[pl.ds(place, LOW)] = buffer[first : first + LOW]
            entry += 1
    lax.fori_loop(0, 2 * requests, merge, 0)
    lax.fori_loop(0, 2 * requests, settle, 0)


def append(info, sent, cache, requests):
    width = cache.shape[2]
    count = len(sent)
    return pl.pallas_call(
        functools.partial(append_body, requests, count),
        out_shape=jax.ShapeDtypeStruct(cache.shape, cache.dtype),
        in_specs=[pl.BlockSpec(memory_space=pltpu.SMEM)]
        + [pl.BlockSpec(memory_space=pltpu.VMEM)] * count
        + [HBM],
        out_specs=HBM,
        input_output_aliases={1 + count: 0},
        scratch_shapes=[
            pltpu.VMEM((requests * LOW, width), jnp.bfloat16),
            pltpu.VMEM((2 * requests, 2, LOW, width), jnp.bfloat16),
            pltpu.SemaphoreType.DMA((2 * requests, 2)),
            pltpu.SemaphoreType.DMA((2 * requests, 2)),
        ],
        compiler_params=pltpu.CompilerParams(vmem_limit_bytes=24 * 1024 * 1024),
        cost_estimate=LIGHT,
        name="append",
    )(info, *sent, cache)


def after(values, earlier):
    return lax.optimization_barrier((values, earlier))[0]


def pass_on(values, axis):
    size = lax.axis_size(axis)
    return lax.ppermute(values, axis, [(i, (i + 1) % size) for i in range(size)])


def swap(values, axis, bits):
    size = lax.axis_size(axis)
    return lax.ppermute(values, axis, [(i, i ^ bits) for i in range(size)])


def on_device(
    tree_input,
    cache,
    page_table,
    lengths,
    parents,
    accept_leaf,
    w_qkv,
    w_out,
    w_up,
    w_down,
    w_draft,
    w_patch,
):
    blocks = lax.axis_size("blk")
    myself = lax.axis_index("blk")
    lines = lax.axis_size("req")
    my_line = lax.axis_index("req")
    width = tree_input.shape[1]
    requests = lengths.shape[1]
    pool_pages = cache.shape[2] // PAGE
    heads = w_draft.shape[0]
    int32 = jnp.int32

    page_row, length_row, leaf_row = page_table[0], lengths[0], accept_leaf[0]
    total_pages = page_row.shape[0]
    npages = (length_row + DEPTH + PAGE - 1) // PAGE
    each = jnp.arange(requests, dtype=int32)
    page_ends = jnp.sum(
        jnp.where(each[None, :] <= each[:, None], npages[None, :], 0), axis=1
    )
    offsets = page_ends - npages
    local = jnp.arange(pool_pages, dtype=int32)
    places = jnp.arange(total_pages, dtype=int32)
    where_at = jnp.sum(
        jnp.where(page_row[None, :] == (myself * pool_pages + local)[:, None], places[None, :], 0),
        axis=1,
    )
    owner_hot = (offsets[None, :] <= where_at[:, None]) & (page_ends[None, :] > where_at[:, None])
    left = jnp.where(
        owner_hot, length_row[None, :] - (where_at[:, None] - offsets[None, :]) * PAGE, 0
    )
    limit = jnp.clip(jnp.sum(left, axis=1), 0, PAGE)
    used = limit > 0
    ranking = jnp.where(used, where_at, total_pages + local)
    rank = jnp.sum((ranking[None, :] < ranking[:, None]).astype(int32), axis=1)
    put = rank[None, :] == local[:, None]
    order = jnp.sum(jnp.where(put, local[None, :], 0), axis=1)
    limit_at = jnp.sum(jnp.where(put, limit[None, :], 0), axis=1)
    holds = (owner_hot & used[:, None]).astype(int32)
    count = jnp.sum(holds, axis=0)
    begin = jnp.sum(jnp.where(each[None, :] < each[:, None], count[None, :], 0), axis=1)
    my_core = myself % 2 if blocks == 8 else jnp.zeros((), int32)
    page_info = jnp.concatenate([order, limit_at, begin, count, my_core.reshape(1)])

    nodes = jnp.arange(TREE, dtype=int32)
    parent_hot = (parents[0][:, None] == nodes[None, :]).astype(jnp.float32)
    leaf_info = jnp.concatenate([leaf_row, myself.reshape(1)])
    if blocks == 8:
        mix_info = myself ^ jnp.asarray((0, 4, 2, 6, 1, 5, 3, 7), int32)
        sent_by = myself ^ jnp.asarray((0, 2, 4, 6, 1, 3, 5, 7), int32)
    else:
        mix_info = jnp.zeros((1,), int32)
        sent_by = each
    others = 2 * ((my_line + lines - jnp.arange(1, lines, dtype=int32)) % lines)
    patch_info = jnp.concatenate(
        [2 * my_line.reshape(1), others + myself % 2, others + (myself ^ 1) % 2]
    )
    level_marks = jnp.asarray(LEVEL_START[1:-1], int32)
    accepted = 1 + jnp.sum((leaf_row[:, None] >= level_marks[None, :]).astype(int32), axis=1)
    block_at = (length_row // LOW * LOW)[:, None] + jnp.arange(2, dtype=int32)[None, :] * LOW
    slot = jnp.minimum(offsets[:, None] + block_at // PAGE, total_pages - 1)
    page = jnp.sum(
        jnp.where(slot[:, :, None] == places[None, None, :], page_row[None, None, :], 0), axis=2
    )
    needed = (length_row + accepted)[:, None] > block_at
    row = jnp.where(
        needed & (page // pool_pages == myself),
        page % pool_pages * PAGE + block_at % PAGE,
        -1,
    )
    shift = block_at - length_row[:, None]
    append_info = jnp.concatenate([row.reshape(-1), shift.reshape(-1), accepted, sent_by])

    tree_all = lax.all_gather(tree_input, "blk", axis=0, tiled=True)
    projected = project(tree_all, w_qkv.T)
    out_rows = w_out.T
    feed_rows = jnp.concatenate([w_up.T, w_down])
    if blocks == 8:
        out_y = swap(after(out_rows, projected), "blk", 4)
        out_x = swap(after(out_rows, projected), "blk", 2)
    half_rows = w_patch.shape[1] // 2
    my_half = lax.dynamic_slice_in_dim(w_patch.T, myself % 2 * half_rows, half_rows, 0)
    ring = [pass_on(after(my_half, projected), "req")]
    projected = lax.all_to_all(projected, "blk", split_axis=0, concat_axis=0, tiled=True)
    projected, page_info, feed_rows = lax.optimization_barrier((projected, page_info, feed_rows))
    projected = projected.transpose(1, 0, 2).reshape(tree_input.shape[0], -1)
    query_all = lax.all_gather(projected[:, :width], "blk", axis=0, tiled=True)
    query_all, ring[0] = lax.optimization_barrier((query_all, ring[0]))
    if blocks == 8:
        query_all, out_y, out_x = lax.optimization_barrier((query_all, out_y, out_x))
        out_xy = swap(out_y, "blk", 2)
        feed_y = swap(after(feed_rows, query_all), "blk", 4)

    if blocks == 8:
        kept, given, cache_copy = attend(page_info, query_all, cache[0], requests, 2)
        kept, given, out_xy = lax.optimization_barrier((kept, given, out_xy))
        parts = merge(kept, swap(given, "blk", 1))
        parts, feed_y = lax.optimization_barrier((parts, feed_y))
        buffers = [out_rows, out_y, out_x, out_xy]
        buffers += [swap(buffer, "blk", 1) for buffer in after(tuple(buffers), kept)]
        feeds = [feed_rows, feed_y]
        feeds.append(swap(after(feed_rows, kept), "blk", 1))
        parts, *buffers = lax.optimization_barrier((parts, *buffers))
        projected = after(projected, parts)
        parts = lax.all_to_all(
            parts,
            "blk",
            split_axis=0,
            concat_axis=0,
            tiled=True,
            axis_index_groups=[list(range(core, blocks, 2)) for core in range(2)],
        )
    else:
        parts, cache_copy = attend(page_info, query_all, cache[0], requests, 1)
        parts = lax.all_to_all(parts, "blk", split_axis=0, concat_axis=0, tiled=True)
        buffers = [lax.all_gather(out_rows, "blk", axis=0, tiled=True)]
        projected = after(projected, parts[0])

    own, sent = tree(leaf_info, projected, parent_hot)
    ring.append(pass_on(after(ring[-1], own), "req"))
    parts, own, append_info, mix_info, patch_info = lax.optimization_barrier(
        (parts, own, append_info, mix_info, patch_info)
    )
    if blocks == 8:
        feeds.append(swap(after(feed_y, own), "blk", 1))
    else:
        halves = [lax.all_gather(one, "blk", axis=0, tiled=True) for one in (w_up.T, w_down)]
        feeds = [jnp.concatenate(halves)]
    mid, mid_normed = mix(mix_info, parts, own, tree_input, sent, buffers)
    sums = [feed(mid_normed, feeds, jnp.float32)]
    if blocks == 8:
        other, sums[0] = lax.optimization_barrier((swap(mid_normed, "blk", 2), sums[0]))
        sent_all = [jnp.concatenate([sent, other[TREE:]])]
        other = feed(other, feeds, jnp.bfloat16)
        sent_all.append(swap(after(sent_all[0], other), "blk", 4))
        ring.append(pass_on(after(ring[-1], other), "req"))
        sums.append(swap(other, "blk", 2))
    else:
        ring.append(pass_on(after(ring[-1], sums[0]), "req"))
    layer_out, draft_rows = finish(mid, sums)
    rows_all = lax.all_gather(draft_rows, "blk", axis=0, tiled=False)
    if blocks == 8:
        rows_all, ring[-1], sent_all[-1] = lax.optimization_barrier(
            (rows_all, ring[-1], sent_all[-1])
        )
        sent_all += [swap(rows, "blk", 1) for rows in after(tuple(sent_all), rows_all)]
    else:
        sent_all = [lax.all_gather(sent, "blk", axis=0, tiled=True)]
    ring += [swap(after(half, rows_all), "blk", 1) for half in ring]

    branch = draft(rows_all, w_draft.transpose(0, 2, 1).reshape(-1, width))
    branch = lax.all_to_all(branch, "blk", split_axis=0, concat_axis=0, tiled=True)
    drafts = patch(patch_info, branch, layer_out, [w_patch.T, *ring], heads)

    cache_new = append(append_info, sent_all, cache_copy, requests)[None]
    return (layer_out, drafts, cache_new)


def solution(mesh):
    in_specs = (
        P(("req", "blk"), None),
        P("req", None, "blk", None),
        P("req", None),
        P("req", None),
        P(("req", "blk"), None),
        P("req", None),
        P(None, "blk"),
        P(None, "blk"),
        P(None, "blk"),
        P("blk", None),
        P(None, None, "blk"),
        P(None, "req"),
    )
    out_specs = (
        P(("req", "blk"), None),
        P(None, ("req", "blk"), None),
        P("req", None, "blk", None),
    )
    return jax.shard_map(
        on_device, mesh=mesh, in_specs=in_specs, out_specs=out_specs, check_vma=False
    )
```
